32 devices in a mesh: space: 8 (over z, x), tm: 4 (over y, core).
Axes of the slice: x: 2, y: 2, z: 4, core: 2. Of those that a mesh axis runs over, the one named last changes fastest.
Arguments:
- right_side: bfloat16 [4, 8, 4, 4, 64, 64], P('tm', 'space'), may hold values from -6 to 6
- batch_order: int32 [32], replicated, may hold values from 0 to 31, each once
- light_diag: bfloat16 [4, 8, 4, 4, 64, 128], P('tm', 'space'), may hold values from -1 to 2
- light_hops: bfloat16 [8, 4, 8, 4, 4, 64, 128], P(None, 'tm', 'space'), may hold values from -0.125 to 0.125
- charm_diag: bfloat16 [4, 8, 4, 4, 64, 128], P('tm', 'space'), may hold values from -1 to 2
- charm_hops: bfloat16 [8, 4, 8, 4, 4, 64, 128], P(None, 'tm', 'space'), may hold values from -0.125 to 0.125
- current_blocks: bfloat16 [4, 8, 4, 4, 64, 128], P('tm', 'space'), may hold values from -0.5 to 0.5
Outputs:
- light_field: bfloat16 [4, 8, 4, 4, 64, 64], P('tm', 'space')
- seq_field: bfloat16 [4, 8, 4, 4, 64, 64], P('tm', 'space')
- margin: float32 [2, 32, 32], replicated
The draws below stay inside these ranges and needn't reach their ends.
All inputs are finite; a program needn't handle non-finite values.
Results may differ from the reference program's by a relative error of at most 0.015.
Values may be sent and summed in bfloat16 or wider, within the bound.
No kernel may reach another device: no remote copies, remote signals or barrier semaphores. Data moves between devices by JAX's collectives and lax.ppermute only.
A program may use at most 64 MiB of HBM per device.

```python
import math
import jax
import jax.numpy as jnp
from jax import lax

NC = 64
COLS = 32
LX = 4
LY = 4
SWEEPS = 4
NZ = 8
NT = 4


def block_draw(key, mass_term):
    block_shape = (NT, NZ, LX, LY, NC, NC)
    spread = 0.3 / math.sqrt(NC)
    key_real, key_imag = jax.random.split(key)
    real_part = jnp.clip(jax.random.normal(key_real, block_shape, jnp.float32), -5.0, 5.0) * spread
    imag_part = jnp.clip(jax.random.normal(key_imag, block_shape, jnp.float32), -5.0, 5.0) * spread
    identity = jnp.eye(NC, dtype=jnp.float32) * mass_term
    return jnp.concatenate([identity + real_part, imag_part], axis=-1).astype(jnp.bfloat16)


def draw_light_diag(key, part):
    return block_draw(jax.random.fold_in(key, 11), 1.0)


def draw_charm_diag(key, part):
    return block_draw(jax.random.fold_in(key, 23), 0.9)


def shard_levels(rng, extent, pieces, low, high):
    loudness, own = 1.0, jax.random.fold_in(rng, 6)
    for dim, blocks in pieces:
        draws = jnp.exp(jax.random.uniform(jax.random.fold_in(own, dim), (blocks,), jnp.float32, low / len(pieces), high / len(pieces)))
        loudness = loudness * jnp.repeat(draws, extent[dim] // blocks).reshape([-1 if axis == dim else 1 for axis in range(len(extent))])
    return loudness


def noise(own_key, dims, deviation, reach, pieces=(), held_as=jnp.bfloat16):
    entries = jax.random.normal(own_key, dims, jnp.float32) * deviation
    if len(pieces) > 0:
        entries = shard_levels(own_key, dims, pieces, -0.22, 0.18) * entries
    return jnp.clip(entries, min=-reach, max=reach).astype(held_as)


def setup_inputs(seed: int = 0) -> dict:
    arg_keys = jax.random.split(jax.random.key(seed), 8)
    return {
        "right_side": noise(arg_keys[0], (NT, NZ, LX, LY, NC, 2 * COLS), 1.0, 6.0, ((0, 4), (1, 8))),
        "batch_order": jax.random.permutation(arg_keys[1], COLS).astype(jnp.int32),
        "light_diag": draw_light_diag(jax.random.fold_in(arg_keys[7], 71), 0),
        "light_hops": noise(arg_keys[3], (8, NT, NZ, LX, LY, NC, 2 * NC), (36 * NC) ** -0.5, 0.125, ((1, 4), (2, 8))),
        "charm_diag": draw_charm_diag(jax.random.fold_in(arg_keys[7], 71), 0),
        "charm_hops": noise(arg_keys[5], (8, NT, NZ, LX, LY, NC, 2 * NC), (40 * NC) ** -0.5, 0.125, ((1, 4), (2, 8))),
        "current_blocks": noise(arg_keys[6], (NT, NZ, LX, LY, NC, 2 * NC), (2 * NC) ** -0.5, 0.5, ((0, 4), (1, 8))),
    }


def expand(spinor):
    columns = spinor.shape[-1] // 2
    real_part = spinor[..., :columns]
    imag_part = spinor[..., columns:]
    lower = jnp.concatenate([-imag_part, real_part], axis=-1)
    return jnp.concatenate([spinor, lower], axis=-2)

def apply_block(blocks, spinor):
    return jnp.einsum('tzxyij,tzxyjk->tzxyik', blocks.astype(jnp.float32), expand(spinor.astype(jnp.float32)))

def hop_terms(hop_blocks, spinor):
    moves = ((-1, 2), (1, 2), (-1, 3), (1, 3), (-1, 1), (1, 1), (-1, 0), (1, 0))
    accumulated = jnp.zeros(spinor.shape, jnp.float32)
    for number in range(8):
        roll_by, roll_axis = moves[number]
        shifted = jnp.roll(spinor, roll_by, axis=roll_axis)
        accumulated = accumulated + apply_block(hop_blocks[number], shifted)
    return accumulated

def solve_system(diag_inverse, hop_blocks, source):
    spinor = jnp.zeros(source.shape, jnp.bfloat16)
    for sweep_index in range(SWEEPS):
        residue = (source.astype(jnp.float32) + hop_terms(hop_blocks, spinor)).astype(jnp.bfloat16)
        spinor = apply_block(diag_inverse, residue).astype(jnp.bfloat16)
    return spinor

def reference(right_side, batch_order, light_diag, light_hops, charm_diag, charm_hops, current_blocks):
    column_index = jnp.concatenate([batch_order, batch_order + COLS]).astype(jnp.int32)
    source = jnp.take(right_side, column_index, axis=-1)
    light_field = solve_system(light_diag, light_hops, source)
    inserted = apply_block(current_blocks, light_field).astype(jnp.bfloat16)
    seq_field = solve_system(charm_diag, charm_hops, inserted)
    flat_light = light_field.reshape(-1, 2 * COLS)
    flat_seq = seq_field.reshape(-1, 2 * COLS)
    gram = lax.dot_general(flat_light, flat_seq, (((0,), (0,)), ((), ())), preferred_element_type=jnp.float32)
    real_sum = gram[:COLS, :COLS] + gram[COLS:, COLS:]
    imag_sum = gram[:COLS, COLS:] - gram[COLS:, :COLS]
    factor_norm = 1.0 / math.sqrt(NT * NZ * LX * LY * NC)
    margin = jnp.stack([real_sum, imag_sum]) * factor_norm
    return (light_field, seq_field, margin)
```

```python
import functools
import math

import jax
import jax.numpy as jnp
from jax import lax
from jax.experimental import pallas as pl
from jax.experimental.pallas import tpu as pltpu
from jax.sharding import PartitionSpec as P

SWEEPS = 4
F32 = jnp.float32
VMEM = pl.BlockSpec(memory_space=pltpu.VMEM)
SMEM = pl.BlockSpec(memory_space=pltpu.SMEM)


def dot(a, b):
    return jnp.dot(a, b, preferred_element_type=F32)


def widen(field):
    half = field.shape[1] // 2
    re, im = field[:, :half], field[:, half:]
    return jnp.concatenate(
        [field, jnp.concatenate([-im, re], axis=1)], axis=0
    )


def pick(product, sites):
    rows = product.shape[0] // sites
    half = product.shape[1] // 2
    lane = lax.broadcasted_iota(jnp.int32, (rows, 2 * half), 1) % half
    out = product[:rows]
    for y in range(1, sites):
        out = jnp.where(lane >= y * (half // sites), product[y * rows : (y + 1) * rows], out)
    return out


def turn(field, shift):
    half = field.shape[1] // 2
    re, im = field[:, :half].astype(F32), field[:, half:].astype(F32)
    return jnp.concatenate(
        [pltpu.roll(re, shift % half, 1), pltpu.roll(im, shift % half, 1)], axis=1
    ).astype(field.dtype)


def first_kernel(order, rhs, diag, source, out):
    lx, ly = rhs.shape[0], rhs.shape[1]
    cols = order.shape[1]
    half = ly * cols
    row = lax.broadcasted_iota(jnp.int32, (2 * cols, 2 * half), 0)
    lane = lax.broadcasted_iota(jnp.int32, (2 * cols, 2 * half), 1)
    wanted = jnp.concatenate([order[...]] * (2 * ly), axis=1)
    wanted = wanted + jnp.where(lane >= half, cols, 0)
    site = (lane % half) // cols
    hot = row == wanted
    places = [jnp.where(hot & (site == y), 1.0, 0.0).astype(jnp.bfloat16) for y in range(ly)]
    for x in range(lx):
        field = dot(rhs[x, 0], places[0])
        for y in range(1, ly):
            field = field + dot(rhs[x, y], places[y])
        field = field.astype(jnp.bfloat16)
        source[x] = field
        out[x] = pick(dot(diag[x], widen(field)), ly).astype(jnp.bfloat16)


def local_kernel(sites, hops, source, field, total):
    lx = field.shape[0]
    cols = field.shape[2] // (2 * sites)
    for x in range(lx):
        here = field[x]
        right = jnp.concatenate(
            [
                widen(field[(x + 1) % lx]),
                widen(field[(x - 1) % lx]),
                widen(turn(here, -cols)),
                widen(turn(here, cols)),
            ],
            axis=0,
        )
        left = jnp.concatenate([hops[e, x] for e in range(4)], axis=1)
        total[x] = source[x].astype(F32) + pick(dot(left, right), sites)


def remote_kernel(sites, which, hops, diag, total, *refs):
    fields, out = refs[:-1], refs[-1]
    lx = out.shape[0]
    for x in range(lx):
        right = jnp.concatenate([widen(f[x]) for f in fields], axis=0)
        left = jnp.concatenate([hops[which[n], x] for n in range(len(fields))], axis=1)
        residue = (total[x] + pick(dot(left, right), sites)).astype(jnp.bfloat16)
        out[x] = pick(dot(diag[x], widen(residue)), sites).astype(jnp.bfloat16)


def insert_kernel(sites, current, diag, field, source, out):
    lx = out.shape[0]
    for x in range(lx):
        inserted = pick(dot(current[x], widen(field[x])), sites).astype(jnp.bfloat16)
        source[x] = inserted
        out[x] = pick(dot(diag[x], widen(inserted)), sites).astype(jnp.bfloat16)


def leave_kernel(field, out):
    lx, ly = out.shape[0], out.shape[1]
    half = field.shape[2] // 2
    cols = half // ly
    row = lax.broadcasted_iota(jnp.int32, (2 * half, 2 * cols), 0)
    lane = lax.broadcasted_iota(jnp.int32, (2 * half, 2 * cols), 1)
    for y in range(ly):
        start = jnp.where(lane >= cols, half - cols, 0) + y * cols
        place = jnp.where(row == lane + start, 1.0, 0.0).astype(jnp.bfloat16)
        for x in range(lx):
            out[x, y] = dot(field[x], place).astype(jnp.bfloat16)


def gram_kernel(sites, left, right, out):
    lx, comps, width = left.shape
    half = width // 2
    cols = half // sites
    a = left[...].reshape(lx * comps, width)
    b = right[...].reshape(lx * comps, width)
    full = lax.dot_general(a, b, (((0,), (0,)), ((), ())), preferred_element_type=F32)
    real = full[:half, :half] + full[half:, half:]
    imag = full[:half, half:] - full[half:, :half]
    lane = lax.broadcasted_iota(jnp.int32, (cols, half), 1) // cols
    parts = []
    for m in (real, imag):
        folded = m[:cols]
        for y in range(1, sites):
            folded = jnp.where(lane == y, m[y * cols : (y + 1) * cols], folded)
        parts.append(folded)
    out[0] = parts[0]
    out[1] = parts[1]


def call(kernel, outs, cost, *args, smem=()):
    flops, moved = cost
    return pl.pallas_call(
        kernel,
        out_shape=outs,
        in_specs=[SMEM if i in smem else VMEM for i in range(len(args))],
        out_specs=jax.tree.map(lambda _: VMEM, outs),
        compiler_params=pltpu.CompilerParams(vmem_limit_bytes=24 * 2**20),
        cost_estimate=pl.CostEstimate(flops=flops, bytes_accessed=moved, transcendentals=0),
    )(*args)


def swaps(axis):
    count = lax.axis_size(axis)
    if count % 2:
        return (
            [(i, (i - 1) % count) for i in range(count)],
            [(i, (i + 1) % count) for i in range(count)],
        )
    near = [(i, i ^ 1) for i in range(count)]
    far = [(i, (i + 1 if i % 2 else i - 1) % count) for i in range(count)]
    return near, far


def parity(axis):
    return lax.axis_index(axis) % 2 if lax.axis_size(axis) % 2 == 0 else jnp.int32(0)


def exchange(field):
    near_s, far_s = swaps("space")
    near_t, far_t = swaps("tm")
    y = lax.ppermute(field, "tm", far_t)
    c = lax.ppermute(field, "tm", near_t)
    w = lax.ppermute(field, "space", far_s)
    e = lax.ppermute(field, "space", near_s)
    return e, w, c, y


def total_sum(value):
    for axis in ("tm", "space"):
        count = lax.axis_size(axis)
        if count & (count - 1):
            value = lax.psum(value, axis)
            continue
        step = 1
        while step < count:
            value = value + lax.ppermute(value, axis, [(i, i ^ step) for i in range(count)])
            step *= 2
    return value


def body(right_side, batch_order, light_diag, light_hops, charm_diag, charm_hops, current_blocks):
    lt, lz, lx, ly, comps, wide = right_side.shape
    assert lt == 1 and lz == 1
    cols = wide // 2
    rows = ly * comps
    rhs = right_side.reshape(lx, ly, comps, wide)
    order = batch_order.reshape(1, cols)
    light_p, charm_p, current = (a.reshape(lx, rows, 2 * comps) for a in (light_diag, charm_diag, current_blocks))
    light_h, charm_h = (a.reshape(8, lx, rows, 2 * comps) for a in (light_hops, charm_hops))
    shape = (lx, comps, 2 * ly * cols)
    field_t = jax.ShapeDtypeStruct(shape, jnp.bfloat16)
    total_t = jax.ShapeDtypeStruct(shape, F32)
    odd_s, odd_t = parity("space"), parity("tm")
    which = jnp.stack([4 + odd_s, 5 - odd_s, 6 + odd_t, 7 - odd_t]).astype(jnp.int32)
    unit = 2 * lx * rows * 2 * comps * 2 * ly * cols

    def sweeps(hops, diag, source, field):
        for _ in range(SWEEPS - 1):
            got = exchange(field)
            total = call(
                functools.partial(local_kernel, ly), total_t, (4 * unit, 2 * 2**20), hops, source, field
            )
            field = call(
                functools.partial(remote_kernel, ly), field_t, (5 * unit, 2 * 2**20), which, hops, diag, total, *got,
                smem=(0,),
            )
        return field

    source, field = call(first_kernel, (field_t, field_t), (2 * unit, 2**20), order, rhs, light_p)
    light = sweeps(light_h, light_p, source, field)
    inserted, field = call(
        functools.partial(insert_kernel, ly), (field_t, field_t), (2 * unit, 2**20), current, charm_p, light
    )
    seq = sweeps(charm_h, charm_p, inserted, field)
    part = call(
        functools.partial(gram_kernel, ly),
        jax.ShapeDtypeStruct((2, cols, ly * cols), F32),
        (unit, 2**20),
        light,
        seq,
    )
    out_t = jax.ShapeDtypeStruct((lx, ly, comps, wide), jnp.bfloat16)
    light_out = call(leave_kernel, out_t, (unit, 2**20), light)
    seq_out = call(leave_kernel, out_t, (unit, 2**20), seq)
    summed = total_sum(part.reshape(2, cols, ly, cols).sum(axis=2))
    site_count = lx * ly * lax.axis_size("space") * lax.axis_size("tm")
    return (
        light_out.reshape(right_side.shape),
        seq_out.reshape(right_side.shape),
        summed * (1.0 / math.sqrt(site_count * comps)),
    )


def solution(mesh):
    site = P("tm", "space", None, None, None, None)
    hops = P(None, "tm", "space", None, None, None, None)
    return jax.shard_map(
        body,
        mesh=mesh,
        in_specs=(site, P(), site, hops, site, hops, site),
        out_specs=(site, site, P()),
        check_vma=False,
    )
```

```python
import functools
import math

import jax
import jax.numpy as jnp
from jax import lax
from jax.experimental import pallas as pl
from jax.experimental.pallas import tpu as pltpu
from jax.sharding import PartitionSpec as P

SWEEPS = 4
F32 = jnp.float32
BF16 = jnp.bfloat16
VMEM = pl.BlockSpec(memory_space=pltpu.VMEM)
HBM = pl.BlockSpec(memory_space=pltpu.HBM)


def dot(a, b):
    return jnp.dot(a, b, preferred_element_type=F32)


def widen(field):
    half = field.shape[1] // 2
    re, im = field[:, :half], field[:, half:]
    return jnp.concatenate(
        [field, jnp.concatenate([-im, re], axis=1)], axis=0
    )


def pick(product, sites):
    rows = product.shape[0] // sites
    half = product.shape[1] // 2
    lane = lax.broadcasted_iota(jnp.int32, (rows, 2 * half), 1) % half
    out = product[:rows]
    for y in range(1, sites):
        out = jnp.where(lane >= y * (half // sites), product[y * rows : (y + 1) * rows], out)
    return out


def turn(field, shift):
    half = field.shape[1] // 2
    re, im = field[:, :half].astype(F32), field[:, half:].astype(F32)
    return jnp.concatenate(
        [pltpu.roll(re, shift % half, 1), pltpu.roll(im, shift % half, 1)], axis=1
    ).astype(field.dtype)


def toward(axes):
    odd = [lax.rem(lax.axis_index(name), 2) if paired else 0 for name, paired in axes]
    return 4 + odd[0], 5 - odd[0], 6 + odd[1], 7 - odd[1]


def hop_loads(axes, hops, local, remote, sems):
    loads = [pltpu.make_async_copy(hops.at[e], local.at[e], sems.at[e]) for e in range(4)]
    return loads + [
        pltpu.make_async_copy(hops.at[e], remote.at[n], sems.at[4 + n]) for n, e in enumerate(toward(axes))
    ]


def load_kernel(axes, hops, local, remote, sems):
    loads = hop_loads(axes, hops, local, remote, sems)
    for load in loads:
        load.start()
    for load in loads:
        load.wait()


def first_kernel(
    axes, order_hbm, rhs_hbm, diag_hbm, hops, source, out, diag, local, remote, order, rhs, sems, hop_sems
):
    copies = [
        pltpu.make_async_copy(order_hbm, order, sems.at[0]),
        pltpu.make_async_copy(rhs_hbm, rhs, sems.at[1]),
        pltpu.make_async_copy(diag_hbm, diag, sems.at[2]),
    ]
    loads = hop_loads(axes, hops, local, remote, hop_sems)
    for copy in copies + loads:
        copy.start()
    lx, ly = rhs.shape[0], rhs.shape[1]
    cols = order.shape[1]
    half = ly * cols
    row = lax.broadcasted_iota(jnp.int32, (2 * cols, 2 * half), 0)
    lane = lax.broadcasted_iota(jnp.int32, (2 * cols, 2 * half), 1)
    copies[0].wait()
    wanted = jnp.concatenate([order[...]] * (2 * ly), axis=1)
    wanted = wanted + jnp.where(lane >= half, cols, 0)
    site = (lane % half) // cols
    hot = row == wanted
    places = [jnp.where(hot & (site == y), 1.0, 0.0).astype(BF16) for y in range(ly)]
    copies[1].wait()
    fields = []
    for x in range(lx):
        field = dot(rhs[x, 0], places[0])
        for y in range(1, ly):
            field = field + dot(rhs[x, y], places[y])
        fields.append(field.astype(BF16))
        source[x] = fields[x]
    copies[2].wait()
    for x in range(lx):
        out[x] = pick(dot(diag[x], widen(fields[x])), ly).astype(BF16)
    for load in loads:
        load.wait()


def local_kernel(sites, hops, source, field, residue):
    lx = field.shape[0]
    cols = field.shape[2] // (2 * sites)
    for x in range(lx):
        here = field[x]
        right = jnp.concatenate(
            [
                widen(field[(x + 1) % lx]),
                widen(field[(x - 1) % lx]),
                widen(turn(here, -cols)),
                widen(turn(here, cols)),
            ],
            axis=0,
        )
        left = jnp.concatenate([hops[e, x] for e in range(4)], axis=1)
        residue[x] = (source[x].astype(F32) + pick(dot(left, right), sites)).astype(BF16)


def blend_kernel(sites, remote, diag, out):
    lx, rows, wide = diag.shape
    comps = rows // sites
    row = lax.broadcasted_iota(jnp.int32, (wide, wide), 0)
    lane = lax.broadcasted_iota(jnp.int32, (wide, wide), 1)
    move = jnp.where(row == lane - comps, 1.0, jnp.where(row == lane + comps, -1.0, 0.0)).astype(BF16)
    for e in range(0, 4, 2):
        for x in range(lx):
            first, second = remote[e, x], remote[e + 1, x]
            low_first, low_second = dot(first, move).astype(BF16), dot(second, move).astype(BF16)
            for y in range(sites):
                at = slice(y * comps, (y + 1) * comps)
                right = jnp.concatenate(
                    [
                        jnp.concatenate([first[at], second[at]], axis=1),
                        jnp.concatenate([low_first[at], low_second[at]], axis=1),
                    ],
                    axis=0,
                )
                both = dot(diag[x, at], right).astype(BF16)
                out[e, x, at] = both[:, :wide]
                out[e + 1, x, at] = both[:, wide:]


def settle_kernel(sites, diag, residue, total):
    for x in range(residue.shape[0]):
        total[x] = pick(dot(diag[x], widen(residue[x])), sites)


def after_kernel(_, token, out):
    out[...] = token[...]


def add_kernel(sites, places, blended, token, total, *refs):
    fields, out = refs[:-1], refs[-1]
    for x in range(out.shape[0]):
        right = jnp.concatenate([widen(f[x]) for f in fields], axis=0)
        left = jnp.concatenate([blended[n, x] for n in places], axis=1)
        out[x] = (total[x] + pick(dot(left, right), sites)).astype(out.dtype)


def insert_kernel(sites, current, diag, field, source, out):
    lx = out.shape[0]
    inserted = [pick(dot(current[x], widen(field[x])), sites).astype(BF16) for x in range(lx)]
    for x in range(lx):
        source[x] = inserted[x]
        out[x] = pick(dot(diag[x], widen(inserted[x])), sites).astype(BF16)


def leave_kernel(*refs):
    refs, token = refs[:-1], refs[-1]
    token[...] = jnp.zeros_like(token)
    count = len(refs) // 2
    lx, ly, comps, wide = refs[count].shape
    half = refs[0].shape[2] // 2
    cols = wide // 2
    row = lax.broadcasted_iota(jnp.int32, (2 * half, wide), 0)
    lane = lax.broadcasted_iota(jnp.int32, (2 * half, wide), 1)
    start = jnp.where(lane >= cols, half - cols, 0)
    for field, out in zip(refs[:count], refs[count:], strict=True):
        whole = field[...].reshape(lx * comps, 2 * half)
        for y in range(ly):
            place = jnp.where(row == lane + start + y * cols, 1.0, 0.0).astype(BF16)
            out[:, y] = dot(whole, place).astype(BF16).reshape(lx, comps, wide)


def gram_kernel(sites, left, right, out):
    lx, comps, width = left.shape
    half = width // 2
    cols = half // sites
    a = left[...].reshape(lx * comps, width)
    b = right[...].reshape(lx * comps, width)
    full = lax.dot_general(a, b, (((0,), (0,)), ((), ())), preferred_element_type=F32)
    real = full[:half, :half] + full[half:, half:]
    imag = full[:half, half:] - full[half:, :half]
    group = lax.broadcasted_iota(jnp.int32, (cols, half), 1) // cols
    sums = []
    for m in (real, imag):
        folded = m[:cols]
        for y in range(1, sites):
            folded = jnp.where(group == y, m[y * cols : (y + 1) * cols], folded)
        total = folded
        for y in range(1, sites):
            total = total + pltpu.roll(folded, y * cols, 1)
        sums.append(total)
    out[...] = jnp.where(group == 0, sums[0], jnp.where(group == 1, sums[1], 0.0))


def margin_kernel(factor, summed, _, out):
    cols = out.shape[1]
    scaled = summed[...] * factor
    out[0] = scaled[:, :cols]
    out[1] = pltpu.roll(scaled, scaled.shape[1] - cols, 1)[:, :cols]


def call(kernel, outs, cost, *args, far=(), scratch=()):
    flops, moved = cost
    args = [pltpu.with_memory_space_constraint(a, pltpu.HBM) if i in far else a for i, a in enumerate(args)]
    return pl.pallas_call(
        kernel,
        out_shape=outs,
        in_specs=[HBM if i in far else VMEM for i in range(len(args))],
        out_specs=jax.tree.map(lambda _: VMEM, outs),
        scratch_shapes=scratch,
        compiler_params=pltpu.CompilerParams(vmem_limit_bytes=24 * 2**20),
        cost_estimate=pl.CostEstimate(flops=flops, bytes_accessed=moved, transcendentals=0),
    )(*args)


def swaps(axis):
    count = lax.axis_size(axis)
    if count % 2:
        return (
            [(i, (i - 1) % count) for i in range(count)],
            [(i, (i + 1) % count) for i in range(count)],
        )
    near = [(i, i ^ 1) for i in range(count)]
    far = [(i, (i + 1 if i % 2 else i - 1) % count) for i in range(count)]
    return near, far


def total_sum(value):
    spaces, times = lax.axis_size("space"), lax.axis_size("tm")
    if (spaces & (spaces - 1)) or (times & (times - 1)):
        return lax.psum(value, ("space", "tm"))

    def swap(mask):
        target = [(s ^ mask[0]) * times + (t ^ mask[1]) for s in range(spaces) for t in range(times)]
        return lax.ppermute(value, ("space", "tm"), list(enumerate(target)))

    cross = 1 if times > 1 else 0
    steps = [(0, 1 << k) for k in range(1, times.bit_length() - 1)]
    steps[1:1] = [(1 << k, 0) for k in range(spaces.bit_length() - 1)]
    if cross:
        value = value + swap((0, 1))
    for k in range(0, len(steps), 2):
        pair = steps[k : k + 2]
        if len(pair) == 2:
            pair.append((pair[0][0] ^ pair[1][0], pair[0][1] ^ pair[1][1]))
        value = sum([swap((s, t ^ cross)) for s, t in pair], value)
    return value


def body(right_side, batch_order, light_diag, light_hops, charm_diag, charm_hops, current_blocks):
    lt, lz, lx, ly, comps, wide = right_side.shape
    assert lt == 1 and lz == 1
    cols = wide // 2
    rows = ly * comps
    rhs = right_side.reshape(lx, ly, comps, wide)
    order = batch_order.reshape(1, cols)
    light_p, charm_p, current = (a.reshape(lx, rows, 2 * comps) for a in (light_diag, charm_diag, current_blocks))
    light_h, charm_h = (a.reshape(8, lx, rows, 2 * comps) for a in (light_hops, charm_hops))
    shape = (lx, comps, 2 * ly * cols)
    field_t = jax.ShapeDtypeStruct(shape, BF16)
    total_t = jax.ShapeDtypeStruct(shape, F32)
    axes = tuple((name, lax.axis_size(name) % 2 == 0) for name in ("space", "tm"))
    unit = 2 * lx * rows * 2 * comps * 2 * ly * cols

    blended_t = jax.ShapeDtypeStruct((4, lx, rows, 2 * comps), BF16)
    near_s, far_s = swaps("space")
    near_t, far_t = swaps("tm")

    token_t = jax.ShapeDtypeStruct((8, 128), F32)

    def sweeps(local, remote, diag, source, field):
        blended = call(functools.partial(blend_kernel, ly), blended_t, (4 * unit, 2**22), remote, diag)
        token = jnp.zeros(token_t.shape, F32)
        for _ in range(SWEEPS - 1):
            y = lax.ppermute(field, "tm", far_t)
            c = lax.ppermute(field, "tm", near_t)
            w = lax.ppermute(field, "space", far_s)
            e = lax.ppermute(field, "space", near_s)
            residue = call(functools.partial(local_kernel, ly), field_t, (4 * unit, 2**21), local, source, field)
            total = call(functools.partial(settle_kernel, ly), total_t, (unit, 2**20), diag, residue)
            for arrived in (e, w):
                token = call(after_kernel, token_t, (0, 2**24), arrived, token)
            field = call(
                functools.partial(add_kernel, ly, (0, 1, 3, 2)), field_t, (4 * unit, 2**20), blended, token, total, e, w, y, c
            )
        return field

    results = (field_t, field_t, jax.ShapeDtypeStruct(light_p.shape, BF16), blended_t, blended_t)
    source, field, light_p, local, remote = call(
        functools.partial(first_kernel, axes), results, (2 * unit, 2**20), order, rhs, light_p, light_h,
        far=(0, 1, 2, 3),
        scratch=(
            pltpu.VMEM(order.shape, jnp.int32),
            pltpu.VMEM(rhs.shape, BF16),
            pltpu.SemaphoreType.DMA((3,)),
            pltpu.SemaphoreType.DMA((8,)),
        ),
    )
    light = sweeps(local, remote, light_p, source, field)
    local, remote = call(
        functools.partial(load_kernel, axes), (blended_t, blended_t), (0, 2**22), charm_h, far=(0,),
        scratch=(pltpu.SemaphoreType.DMA((8,)),),
    )
    inserted, field = call(
        functools.partial(insert_kernel, ly), (field_t, field_t), (2 * unit, 2**20), current, charm_p, light
    )
    seq = sweeps(local, remote, charm_p, inserted, field)
    part = call(
        functools.partial(gram_kernel, ly), jax.ShapeDtypeStruct((cols, ly * cols), F32), (unit, 2**20), light, seq
    )
    out_t = jax.ShapeDtypeStruct((lx, ly, comps, wide), BF16)
    light_out, seq_out, token = call(leave_kernel, (out_t, out_t, token_t), (unit, 2**22), light, seq)
    summed = total_sum(part)
    site_count = lx * ly * lax.axis_size("space") * lax.axis_size("tm")
    factor = 1.0 / math.sqrt(site_count * comps)
    margin = call(
        functools.partial(margin_kernel, factor), jax.ShapeDtypeStruct((2, cols, cols), F32), (2**14, 2**14), summed, token
    )
    return light_out.reshape(right_side.shape), seq_out.reshape(right_side.shape), margin


def solution(mesh):
    site = P("tm", "space", None, None, None, None)
    hops = P(None, "tm", "space", None, None, None, None)
    return jax.shard_map(
        body,
        mesh=mesh,
        in_specs=(site, P(), site, hops, site, hops, site),
        out_specs=(site, site, P()),
        check_vma=False,
    )
```

```python
import functools
import math

import jax
import jax.numpy as jnp
from jax import lax
from jax.experimental import pallas as pl
from jax.experimental.pallas import tpu as pltpu
from jax.sharding import PartitionSpec as P

SWEEPS = 4
F32 = jnp.float32
BF16 = jnp.bfloat16
VMEM = pl.BlockSpec(memory_space=pltpu.VMEM)
HBM = pl.BlockSpec(memory_space=pltpu.HBM)


def dot(a, b):
    return jnp.dot(a, b, preferred_element_type=F32)


def widen(field):
    half = field.shape[1] // 2
    re, im = field[:, :half], field[:, half:]
    return jnp.concatenate(
        [field, jnp.concatenate([-im, re], axis=1)], axis=0
    )


def pick(product, sites):
    rows = product.shape[0] // sites
    half = product.shape[1] // 2
    lane = lax.broadcasted_iota(jnp.int32, (rows, 2 * half), 1) % half
    out = product[:rows]
    for y in range(1, sites):
        out = jnp.where(lane >= y * (half // sites), product[y * rows : (y + 1) * rows], out)
    return out


def turn(field, shift):
    half = field.shape[1] // 2
    re, im = field[:, :half].astype(F32), field[:, half:].astype(F32)
    return jnp.concatenate(
        [pltpu.roll(re, shift % half, 1), pltpu.roll(im, shift % half, 1)], axis=1
    ).astype(field.dtype)


def toward(axes):
    odd = [lax.rem(lax.axis_index(name), 2) if paired else 0 for name, paired in axes]
    return 4 + odd[0], 5 - odd[0], 6 + odd[1], 7 - odd[1]


def hop_loads(axes, hops, local, remote, sems):
    loads = [pltpu.make_async_copy(hops.at[e], local.at[e], sems.at[e]) for e in range(4)]
    return loads + [
        pltpu.make_async_copy(hops.at[e], remote.at[n], sems.at[4 + n]) for n, e in enumerate(toward(axes))
    ]


def load_kernel(axes, hops, local, remote, sems):
    loads = hop_loads(axes, hops, local, remote, sems)
    for load in loads:
        load.start()
    for load in loads:
        load.wait()


def first_kernel(order_hbm, rhs_hbm, diag_hbm, source, out, diag, order, rhs, sems):
    copies = [
        pltpu.make_async_copy(order_hbm, order, sems.at[0]),
        pltpu.make_async_copy(rhs_hbm, rhs, sems.at[1]),
        pltpu.make_async_copy(diag_hbm, diag, sems.at[2]),
    ]
    for copy in copies:
        copy.start()
    lx, ly = rhs.shape[0], rhs.shape[1]
    cols = order.shape[1]
    half = ly * cols
    row = lax.broadcasted_iota(jnp.int32, (2 * cols, 2 * half), 0)
    lane = lax.broadcasted_iota(jnp.int32, (2 * cols, 2 * half), 1)
    copies[0].wait()
    wanted = jnp.concatenate([order[...]] * (2 * ly), axis=1)
    wanted = wanted + jnp.where(lane >= half, cols, 0)
    site = (lane % half) // cols
    hot = row == wanted
    places = [jnp.where(hot & (site == y), 1.0, 0.0).astype(BF16) for y in range(ly)]
    copies[1].wait()
    fields = []
    for x in range(lx):
        field = dot(rhs[x, 0], places[0])
        for y in range(1, ly):
            field = field + dot(rhs[x, y], places[y])
        fields.append(field.astype(BF16))
        source[x] = fields[x]
    copies[2].wait()
    for x in range(lx):
        out[x] = pick(dot(diag[x], widen(fields[x])), ly).astype(BF16)


def local_kernel(sites, hops, source, field, residue):
    lx = field.shape[0]
    cols = field.shape[2] // (2 * sites)
    for x in range(lx):
        here = field[x]
        right = jnp.concatenate(
            [
                widen(field[(x + 1) % lx]),
                widen(field[(x - 1) % lx]),
                widen(turn(here, -cols)),
                widen(turn(here, cols)),
            ],
            axis=0,
        )
        left = jnp.concatenate([hops[e, x] for e in range(4)], axis=1)
        residue[x] = (source[x].astype(F32) + pick(dot(left, right), sites)).astype(BF16)


def times_i(wide):
    row = lax.broadcasted_iota(jnp.int32, (wide, wide), 0)
    lane = lax.broadcasted_iota(jnp.int32, (wide, wide), 1)
    half = wide // 2
    return jnp.where(row == lane - half, 1.0, jnp.where(row == lane + half, -1.0, 0.0)).astype(BF16)


def blend_kernel(sites, remote, diag, out):
    count = remote.shape[0]
    lx, rows, wide = diag.shape
    comps = rows // sites
    move = times_i(wide)
    step = 2 if count % 2 == 0 else 1
    for e in range(0, count, step):
        for x in range(lx):
            blocks = [remote[e + n, x] for n in range(step)]
            lower = [dot(block, move).astype(BF16) for block in blocks]
            for y in range(sites):
                at = slice(y * comps, (y + 1) * comps)
                right = jnp.concatenate(
                    [
                        jnp.concatenate([block[at] for block in blocks], axis=1),
                        jnp.concatenate([block[at] for block in lower], axis=1),
                    ],
                    axis=0,
                )
                product = dot(diag[x, at], right).astype(BF16)
                for n in range(step):
                    out[e + n, x, at] = product[:, n * wide : (n + 1) * wide]


def settle_kernel(sites, diag, residue, total):
    for x in range(residue.shape[0]):
        total[x] = pick(dot(diag[x], widen(residue[x])), sites)


def after_kernel(_, token, out):
    out[...] = token[...]


def add_remote(sites, places, blended, total, fields, x):
    right = jnp.concatenate([widen(f[x]) for f in fields], axis=0)
    left = jnp.concatenate([blended[n, x] for n in places], axis=1)
    return (total[x] + pick(dot(left, right), sites)).astype(BF16)


def add_kernel(sites, places, blended, token, total, *refs):
    fields, out = refs[:-1], refs[-1]
    for x in range(out.shape[0]):
        out[x] = add_remote(sites, places, blended, total, fields, x)


def add_insert_kernel(sites, places, blended, token, total, *refs):
    fields, both, out, start = refs[:-3], refs[-3], refs[-2], refs[-1]
    new = [add_remote(sites, places, blended, total, fields, x) for x in range(out.shape[0])]
    for x in range(out.shape[0]):
        out[x] = new[x]
        start[x] = pick(dot(both[x], widen(new[x])), sites).astype(BF16)


def add_gram_kernel(sites, places, blended, token, total, *refs):
    fields, left, out, gram = refs[:-3], refs[-3], refs[-2], refs[-1]
    new = [add_remote(sites, places, blended, total, fields, x) for x in range(out.shape[0])]
    for x in range(out.shape[0]):
        out[x] = new[x]
    gram[...] = packed_gram(sites, left[...], jnp.concatenate(new, axis=0))


def insert_kernel(sites, current, field, source):
    for x in range(source.shape[0]):
        source[x] = pick(dot(current[x], widen(field[x])), sites).astype(BF16)


def turn_over_kernel(field, out):
    lx, comps, width = field.shape
    out[...] = field[...].reshape(lx * comps, width).astype(F32).T.astype(BF16)


def leave_kernel(*refs):
    refs, token = refs[:-1], refs[-1]
    token[...] = jnp.zeros_like(token)
    count = len(refs) // 2
    lx, ly, comps, wide = refs[count].shape
    half = refs[0].shape[2] // 2
    cols = wide // 2
    row = lax.broadcasted_iota(jnp.int32, (2 * half, wide), 0)
    lane = lax.broadcasted_iota(jnp.int32, (2 * half, wide), 1)
    start = jnp.where(lane >= cols, half - cols, 0)
    for field, out in zip(refs[:count], refs[count:], strict=True):
        whole = field[...].reshape(lx * comps, 2 * half)
        for y in range(ly):
            place = jnp.where(row == lane + start + y * cols, 1.0, 0.0).astype(BF16)
            out[:, y] = dot(whole, place).astype(BF16).reshape(lx, comps, wide)


def packed_gram(sites, left, right):
    half = left.shape[0] // 2
    cols = half // sites
    full = dot(left, right)
    real = full[:half, :half] + full[half:, half:]
    imag = full[:half, half:] - full[half:, :half]
    group = lax.broadcasted_iota(jnp.int32, (cols, half), 1) // cols
    sums = []
    for m in (real, imag):
        folded = m[:cols]
        for y in range(1, sites):
            folded = jnp.where(group == y, m[y * cols : (y + 1) * cols], folded)
        total = folded
        for y in range(1, sites):
            total = total + pltpu.roll(folded, y * cols, 1)
        sums.append(total)
    top = group[: cols // 2]
    packed = jnp.where(top == 0, sums[0][: cols // 2], sums[1][: cols // 2])
    packed = jnp.where(top == 2, sums[0][cols // 2 :], packed)
    return jnp.where(top == 3, sums[1][cols // 2 :], packed)


def margin_kernel(factor, summed, _, out):
    cols = out.shape[1]
    scaled = summed[...] * factor
    for part in range(4):
        rows = slice(part // 2 * (cols // 2), (part // 2 + 1) * (cols // 2))
        out[part % 2, rows] = (pltpu.roll(scaled, scaled.shape[1] - part * cols, 1) if part else scaled)[:, :cols]


def call(kernel, outs, cost, *args, far=(), scratch=()):
    flops, moved = cost
    args = [pltpu.with_memory_space_constraint(a, pltpu.HBM) if i in far else a for i, a in enumerate(args)]
    return pl.pallas_call(
        kernel,
        out_shape=outs,
        in_specs=[HBM if i in far else VMEM for i in range(len(args))],
        out_specs=jax.tree.map(lambda _: VMEM, outs),
        scratch_shapes=scratch,
        compiler_params=pltpu.CompilerParams(vmem_limit_bytes=24 * 2**20),
        cost_estimate=pl.CostEstimate(flops=flops, bytes_accessed=moved, transcendentals=0),
    )(*args)


def swaps(axis):
    count = lax.axis_size(axis)
    if count % 2:
        return (
            [(i, (i - 1) % count) for i in range(count)],
            [(i, (i + 1) % count) for i in range(count)],
        )
    near = [(i, i ^ 1) for i in range(count)]
    far = [(i, (i + 1 if i % 2 else i - 1) % count) for i in range(count)]
    return near, far


def total_sum(value):
    spaces, times = lax.axis_size("space"), lax.axis_size("tm")
    if (spaces & (spaces - 1)) or (times & (times - 1)):
        return lax.psum(value, ("space", "tm"))

    def swap(mask):
        target = [(s ^ mask[0]) * times + (t ^ mask[1]) for s in range(spaces) for t in range(times)]
        return lax.ppermute(value, ("space", "tm"), list(enumerate(target)))

    cross = 1 if times > 1 else 0
    steps = [(0, 1 << k) for k in range(1, times.bit_length() - 1)]
    steps[1:1] = [(1 << k, 0) for k in range(spaces.bit_length() - 1)]
    if cross:
        value = value + swap((0, 1))
    for k in range(0, len(steps), 2):
        pair = steps[k : k + 2]
        if len(pair) == 2:
            pair.append((pair[0][0] ^ pair[1][0], pair[0][1] ^ pair[1][1]))
        value = sum([swap((s, t ^ cross)) for s, t in pair], value)
    return value


def body(right_side, batch_order, light_diag, light_hops, charm_diag, charm_hops, current_blocks):
    lt, lz, lx, ly, comps, wide = right_side.shape
    assert lt == 1 and lz == 1
    cols = wide // 2
    rows = ly * comps
    rhs = right_side.reshape(lx, ly, comps, wide)
    order = batch_order.reshape(1, cols)
    light_p, charm_p, current = (a.reshape(lx, rows, 2 * comps) for a in (light_diag, charm_diag, current_blocks))
    light_h, charm_h = (a.reshape(8, lx, rows, 2 * comps) for a in (light_hops, charm_hops))
    shape = (lx, comps, 2 * ly * cols)
    field_t = jax.ShapeDtypeStruct(shape, BF16)
    total_t = jax.ShapeDtypeStruct(shape, F32)
    axes = tuple((name, lax.axis_size(name) % 2 == 0) for name in ("space", "tm"))
    unit = 2 * lx * rows * 2 * comps * 2 * ly * cols

    blended_t = jax.ShapeDtypeStruct((4, lx, rows, 2 * comps), BF16)
    near_s, far_s = swaps("space")
    near_t, far_t = swaps("tm")

    token_t = jax.ShapeDtypeStruct((8, 128), F32)

    def sweeps(local, remote, diag, source, field, last, last_t, extra):
        blended = call(functools.partial(blend_kernel, ly), blended_t, (4 * unit, 2**22), remote, diag)
        token = jnp.zeros(token_t.shape, F32)
        for left in reversed(range(SWEEPS - 1)):
            y = lax.ppermute(field, "tm", far_t)
            c = lax.ppermute(field, "tm", near_t)
            w = lax.ppermute(field, "space", far_s)
            e = lax.ppermute(field, "space", near_s)
            if not isinstance(source, jax.Array):
                source = call(functools.partial(insert_kernel, ly), field_t, (unit, 2**20), *source)
            residue = call(functools.partial(local_kernel, ly), field_t, (4 * unit, 2**21), local, source, field)
            total = call(functools.partial(settle_kernel, ly), total_t, (unit, 2**20), diag, residue)
            for arrived in (e, w):
                token = call(after_kernel, token_t, (0, 2**24), arrived, token)
            kernel, outs = (add_kernel, field_t) if left else (last, (field_t, last_t))
            field = call(
                functools.partial(kernel, ly, (0, 1, 3, 2)), outs, (4 * unit, 2**20), blended, token, total, e, w, y, c,
                *(() if left else (extra,)),
            )
        return field

    results = (field_t, field_t, jax.ShapeDtypeStruct(light_p.shape, BF16))
    source, field, light_p = call(
        first_kernel, results, (2 * unit, 2**20), order, rhs, light_p,
        far=(0, 1, 2),
        scratch=(
            pltpu.VMEM(order.shape, jnp.int32),
            pltpu.VMEM(rhs.shape, BF16),
            pltpu.SemaphoreType.DMA((3,)),
        ),
    )

    def load(hops):
        return call(
            functools.partial(load_kernel, axes), (blended_t, blended_t), (0, 2**22), hops, far=(0,),
            scratch=(pltpu.SemaphoreType.DMA((8,)),),
        )

    local, remote = load(light_h)
    one_t = jax.ShapeDtypeStruct((1, *current.shape), BF16)
    both = call(functools.partial(blend_kernel, ly), one_t, (unit, 2**20), current[None], charm_p)[0]
    light, field = sweeps(local, remote, light_p, source, field, add_insert_kernel, field_t, both)
    local, remote = load(charm_h)
    over = call(turn_over_kernel, jax.ShapeDtypeStruct((2 * ly * cols, lx * comps), BF16), (unit, 2**20), light)
    part_t = jax.ShapeDtypeStruct((cols // 2, ly * cols), F32)
    seq, part = sweeps(local, remote, charm_p, (current, light), field, add_gram_kernel, part_t, over)
    out_t = jax.ShapeDtypeStruct((lx, ly, comps, wide), BF16)
    light_out, seq_out, token = call(leave_kernel, (out_t, out_t, token_t), (unit, 2**22), light, seq)
    summed = total_sum(part)
    site_count = lx * ly * lax.axis_size("space") * lax.axis_size("tm")
    factor = 1.0 / math.sqrt(site_count * comps)
    margin = call(
        functools.partial(margin_kernel, factor), jax.ShapeDtypeStruct((2, cols, cols), F32), (2**14, 2**14), summed, token
    )
    return light_out.reshape(right_side.shape), seq_out.reshape(right_side.shape), margin


def solution(mesh):
    site = P("tm", "space", None, None, None, None)
    hops = P(None, "tm", "space", None, None, None, None)
    return jax.shard_map(
        body,
        mesh=mesh,
        in_specs=(site, P(), site, hops, site, hops, site),
        out_specs=(site, site, P()),
        check_vma=False,
    )
```

```python
import functools
import math

import jax
import jax.numpy as jnp
from jax import lax
from jax.experimental import pallas as pl
from jax.experimental.pallas import tpu as pltpu
from jax.sharding import PartitionSpec as P

SWEEPS = 4
F32 = jnp.float32
BF16 = jnp.bfloat16
VMEM = pl.BlockSpec(memory_space=pltpu.VMEM)
HBM = pl.BlockSpec(memory_space=pltpu.HBM)


def dot(a, b):
    return jnp.dot(a, b, preferred_element_type=F32)


def widen(field):
    half = field.shape[1] // 2
    re, im = field[:, :half], field[:, half:]
    return jnp.concatenate(
        [field, jnp.concatenate([-im, re], axis=1)], axis=0
    )


def pick(product, sites):
    rows = product.shape[0] // sites
    half = product.shape[1] // 2
    lane = lax.broadcasted_iota(jnp.int32, (rows, 2 * half), 1) % half
    out = product[:rows]
    for y in range(1, sites):
        out = jnp.where(lane >= y * (half // sites), product[y * rows : (y + 1) * rows], out)
    return out


def turn(field, shift):
    half = field.shape[1] // 2
    re, im = field[:, :half].astype(F32), field[:, half:].astype(F32)
    return jnp.concatenate(
        [pltpu.roll(re, shift % half, 1), pltpu.roll(im, shift % half, 1)], axis=1
    ).astype(field.dtype)


def toward(axes):
    odd = [lax.rem(lax.axis_index(name), 2) if paired else 0 for name, paired in axes]
    return 4 + odd[0], 5 - odd[0], 6 + odd[1], 7 - odd[1]


def hop_loads(axes, hops, local, remote, sems):
    loads = [pltpu.make_async_copy(hops.at[e], local.at[e], sems.at[e]) for e in range(4)]
    return loads + [
        pltpu.make_async_copy(hops.at[e], remote.at[n], sems.at[4 + n]) for n, e in enumerate(toward(axes))
    ]


def load_kernel(axes, hops, local, remote, sems):
    loads = hop_loads(axes, hops, local, remote, sems)
    for load in loads:
        load.start()
    for load in loads:
        load.wait()


def first_kernel(order_hbm, rhs_hbm, diag_hbm, source, out, diag, order, rhs, sems):
    copies = [
        pltpu.make_async_copy(order_hbm, order, sems.at[0]),
        pltpu.make_async_copy(rhs_hbm, rhs, sems.at[1]),
        pltpu.make_async_copy(diag_hbm, diag, sems.at[2]),
    ]
    for copy in copies:
        copy.start()
    lx, ly = rhs.shape[0], rhs.shape[1]
    cols = order.shape[1]
    half = ly * cols
    row = lax.broadcasted_iota(jnp.int32, (2 * cols, 2 * half), 0)
    lane = lax.broadcasted_iota(jnp.int32, (2 * cols, 2 * half), 1)
    copies[0].wait()
    wanted = jnp.concatenate([order[...]] * (2 * ly), axis=1)
    wanted = wanted + jnp.where(lane >= half, cols, 0)
    site = (lane % half) // cols
    hot = row == wanted
    places = [jnp.where(hot & (site == y), 1.0, 0.0).astype(BF16) for y in range(ly)]
    copies[1].wait()
    fields = []
    for x in range(lx):
        field = dot(rhs[x, 0], places[0])
        for y in range(1, ly):
            field = field + dot(rhs[x, y], places[y])
        fields.append(field.astype(BF16))
        source[x] = fields[x]
    copies[2].wait()
    for x in range(lx):
        out[x] = pick(dot(diag[x], widen(fields[x])), ly).astype(BF16)


def local_kernel(sites, hops, source, field, residue):
    lx = field.shape[0]
    cols = field.shape[2] // (2 * sites)
    for x in range(lx):
        here = field[x]
        right = jnp.concatenate(
            [
                widen(field[(x + 1) % lx]),
                widen(field[(x - 1) % lx]),
                widen(turn(here, -cols)),
                widen(turn(here, cols)),
            ],
            axis=0,
        )
        left = jnp.concatenate([hops[e, x] for e in range(4)], axis=1)
        residue[x] = (source[x].astype(F32) + pick(dot(left, right), sites)).astype(BF16)


def times_i(wide):
    row = lax.broadcasted_iota(jnp.int32, (wide, wide), 0)
    lane = lax.broadcasted_iota(jnp.int32, (wide, wide), 1)
    half = wide // 2
    return jnp.where(row == lane - half, 1.0, jnp.where(row == lane + half, -1.0, 0.0)).astype(BF16)


def blend_kernel(sites, remote, diag, out):
    count = remote.shape[0]
    lx, rows, wide = diag.shape
    comps = rows // sites
    move = times_i(wide)
    step = 2 if count % 2 == 0 else 1
    for e in range(0, count, step):
        for x in range(lx):
            blocks = [remote[e + n, x] for n in range(step)]
            lower = [dot(block, move).astype(BF16) for block in blocks]
            for y in range(sites):
                at = slice(y * comps, (y + 1) * comps)
                right = jnp.concatenate(
                    [
                        jnp.concatenate([block[at] for block in blocks], axis=1),
                        jnp.concatenate([block[at] for block in lower], axis=1),
                    ],
                    axis=0,
                )
                product = dot(diag[x, at], right).astype(BF16)
                for n in range(step):
                    out[e + n, x, at] = product[:, n * wide : (n + 1) * wide]


def settle_kernel(sites, diag, residue, total):
    for x in range(residue.shape[0]):
        total[x] = pick(dot(diag[x], widen(residue[x].astype(BF16))), sites)


def after_kernel(_, token, out):
    out[...] = token[...]


def add_kernel(sites, places, blended, token, total, *refs):
    fields, out = refs[:-1], refs[-1]
    for x in range(out.shape[0]):
        right = jnp.concatenate([widen(f[x]) for f in fields], axis=0)
        left = jnp.concatenate([blended[n, x] for n in places], axis=1)
        out[x] = (total[x] + pick(dot(left, right), sites)).astype(BF16)


def adjoint_kernel(sites, over, blended, out):
    width = over.shape[1]
    count, lx, rows, wide = blended.shape
    comps = rows // sites
    row = lax.broadcasted_iota(jnp.int32, (comps, rows), 0)
    spread = jnp.where(row == lax.broadcasted_iota(jnp.int32, (comps, rows), 1) % comps, 1.0, 0.0).astype(BF16)
    half = width // 2
    site = lax.broadcasted_iota(jnp.int32, (width, rows), 0) % half // (half // sites)
    own = site == lax.broadcasted_iota(jnp.int32, (width, rows), 1) // comps
    low = lax.broadcasted_iota(jnp.int32, (half, wide), 1) < comps
    for x in range(0, lx, 2):
        blocks = [jnp.where(own, dot(over[x + k], spread), 0.0).astype(BF16) for k in range(2)]
        at = slice(x // 2 * wide, (x // 2 + 1) * wide)
        for n in range(count):
            one, two = (dot(blocks[k], blended[n, x + k]) for k in range(2))
            re = jnp.where(low, one[:half] + pltpu.roll(one[half:], comps, 1), pltpu.roll(two[:half], comps, 1) + two[half:])
            im = jnp.where(low, one[half:] - pltpu.roll(one[:half], comps, 1), pltpu.roll(two[half:], comps, 1) - two[:half])
            out[n, :half, at] = re.astype(BF16)
            out[n, half:, at] = im.astype(BF16)


def gram_kernel(sites, places, whole, adjoint, token, total, *refs):
    fields, out = refs[:-1], refs[-1]
    left = jnp.concatenate([whole[...]] + [adjoint[n] for n in places], axis=1)
    right = [total[...].astype(BF16)] + [f[...] for f in fields]
    right = jnp.concatenate([f.reshape(-1, f.shape[2]) for f in right], axis=0)
    out[...] = packed_gram(sites, left, right)


def insert_kernel(sites, current, field, source):
    for x in range(source.shape[0]):
        source[x] = pick(dot(current[x], widen(field[x])), sites).astype(BF16)


def turn_over_kernel(field, whole, out):
    lx, comps, width = field.shape
    whole[...] = field[...].reshape(lx * comps, width).astype(F32).T.astype(BF16)
    for x in range(lx):
        out[x] = field[x].astype(F32).T.astype(BF16)


def leave_kernel(*refs):
    refs, token = refs[:-1], refs[-1]
    token[...] = jnp.zeros_like(token)
    count = len(refs) // 2
    lx, ly, comps, wide = refs[count].shape
    half = refs[0].shape[2] // 2
    cols = wide // 2
    row = lax.broadcasted_iota(jnp.int32, (2 * half, wide), 0)
    lane = lax.broadcasted_iota(jnp.int32, (2 * half, wide), 1)
    start = jnp.where(lane >= cols, half - cols, 0)
    for field, out in zip(refs[:count], refs[count:], strict=True):
        whole = field[...].reshape(lx * comps, 2 * half)
        for y in range(ly):
            place = jnp.where(row == lane + start + y * cols, 1.0, 0.0).astype(BF16)
            out[:, y] = dot(whole, place).astype(BF16).reshape(lx, comps, wide)


def packed_gram(sites, left, right):
    half = left.shape[0] // 2
    cols = half // sites
    full = dot(left, right)
    real = full[:half, :half] + full[half:, half:]
    imag = full[:half, half:] - full[half:, :half]
    group = lax.broadcasted_iota(jnp.int32, (cols, half), 1) // cols
    sums = []
    for m in (real, imag):
        folded = m[:cols]
        for y in range(1, sites):
            folded = jnp.where(group == y, m[y * cols : (y + 1) * cols], folded)
        total = folded
        for y in range(1, sites):
            total = total + pltpu.roll(folded, y * cols, 1)
        sums.append(total)
    top = group[: cols // 2]
    packed = jnp.where(top == 0, sums[0][: cols // 2], sums[1][: cols // 2])
    packed = jnp.where(top == 2, sums[0][cols // 2 :], packed)
    return jnp.where(top == 3, sums[1][cols // 2 :], packed)


def margin_kernel(factor, _, token, *refs):
    out = refs[-1]
    cols = out.shape[1]
    scaled = sum([ref[...] for ref in refs[1:-1]], refs[0][...]) * factor
    for part in range(4):
        rows = slice(part // 2 * (cols // 2), (part // 2 + 1) * (cols // 2))
        out[part % 2, rows] = (pltpu.roll(scaled, scaled.shape[1] - part * cols, 1) if part else scaled)[:, :cols]


def call(kernel, outs, cost, *args, far=(), scratch=()):
    flops, moved = cost
    args = [pltpu.with_memory_space_constraint(a, pltpu.HBM) if i in far else a for i, a in enumerate(args)]
    return pl.pallas_call(
        kernel,
        out_shape=outs,
        in_specs=[HBM if i in far else VMEM for i in range(len(args))],
        out_specs=jax.tree.map(lambda _: VMEM, outs),
        scratch_shapes=scratch,
        compiler_params=pltpu.CompilerParams(vmem_limit_bytes=24 * 2**20),
        cost_estimate=pl.CostEstimate(flops=flops, bytes_accessed=moved, transcendentals=0),
    )(*args)


def in_order(arrivals, token):
    for arrived in arrivals:
        token = call(after_kernel, jax.ShapeDtypeStruct(token.shape, token.dtype), (0, 2**24), arrived, token)
    return token


def sum_kernel(token, value, *refs):
    total = value[...]
    for ref in refs[:-1]:
        total = total + ref[...]
    refs[-1][...] = total


def add_up(value, got, aside):
    token = in_order((*aside, *got), jnp.zeros((8, 128), F32))
    return call(sum_kernel, jax.ShapeDtypeStruct(value.shape, F32), (0, 2**14), token, value, *got)


def swaps(axis):
    count = lax.axis_size(axis)
    if count % 2:
        return (
            [(i, (i - 1) % count) for i in range(count)],
            [(i, (i + 1) % count) for i in range(count)],
        )
    near = [(i, i ^ 1) for i in range(count)]
    far = [(i, (i + 1 if i % 2 else i - 1) % count) for i in range(count)]
    return near, far


def total_sum(value, last, aside):
    spaces, times = lax.axis_size("space"), lax.axis_size("tm")
    if (spaces & (spaces - 1)) or (times & (times - 1)):
        return last(lax.psum(value, ("space", "tm")))

    def swap(mask):
        target = [(s ^ mask[0]) * times + (t ^ mask[1]) for s in range(spaces) for t in range(times)]
        return lax.ppermute(value, ("space", "tm"), list(enumerate(target)))

    cross = 1 if times > 1 else 0
    steps = [(0, 1 << k) for k in range(1, times.bit_length() - 1)]
    steps[1:1] = [(1 << k, 0) for k in range(spaces.bit_length() - 1)]
    groups = []
    for k in range(0, len(steps), 2):
        pair = steps[k : k + 2]
        if len(pair) == 2:
            pair.append((pair[0][0] ^ pair[1][0], pair[0][1] ^ pair[1][1]))
        groups.append([(s, t ^ cross) for s, t in reversed(pair)])
    if cross:
        groups.insert(0, [(0, 1)])
    for group in groups[:-1]:
        value = add_up(value, [swap(mask) for mask in group], aside if group == groups[-2] else ())
    return last(value, *[swap(mask) for mask in groups[-1]]) if groups else last(value)


def body(right_side, batch_order, light_diag, light_hops, charm_diag, charm_hops, current_blocks):
    lt, lz, lx, ly, comps, wide = right_side.shape
    assert lt == 1 and lz == 1
    cols = wide // 2
    rows = ly * comps
    rhs = right_side.reshape(lx, ly, comps, wide)
    order = batch_order.reshape(1, cols)
    light_p, charm_p, current = (a.reshape(lx, rows, 2 * comps) for a in (light_diag, charm_diag, current_blocks))
    light_h, charm_h = (a.reshape(8, lx, rows, 2 * comps) for a in (light_hops, charm_hops))
    shape = (lx, comps, 2 * ly * cols)
    field_t = jax.ShapeDtypeStruct(shape, BF16)
    total_t = jax.ShapeDtypeStruct(shape, F32)
    axes = tuple((name, lax.axis_size(name) % 2 == 0) for name in ("space", "tm"))
    unit = 2 * lx * rows * 2 * comps * 2 * ly * cols

    blended_t = jax.ShapeDtypeStruct((4, lx, rows, 2 * comps), BF16)
    near_s, far_s = swaps("space")
    near_t, far_t = swaps("tm")

    token_t = jax.ShapeDtypeStruct((8, 128), F32)

    def sweeps(local, blended, diag, source, field, aside=()):
        token = jnp.zeros(token_t.shape, F32)
        for left in reversed(range(SWEEPS - 1)):
            y = lax.ppermute(field, "tm", far_t)
            c = lax.ppermute(field, "tm", near_t)
            w = lax.ppermute(field, "space", far_s)
            e = lax.ppermute(field, "space", near_s)
            if not isinstance(source, jax.Array):
                source = call(functools.partial(insert_kernel, ly), field_t, (unit, 2**20), *source)
            residue = call(functools.partial(local_kernel, ly), field_t, (4 * unit, 2**21), local, source, field)
            total = call(functools.partial(settle_kernel, ly), total_t, (unit, 2**20), diag, residue)
            token = in_order((*(aside if left == 1 else ()), e, w), token)

            def finish(kernel, outs, matrices, token, total, got=(e, w, y, c)):
                return call(
                    functools.partial(kernel, ly, (0, 1, 3, 2)), outs, (4 * unit, 2**20), *matrices, token, total, *got
                )

            if left:
                field = finish(add_kernel, field_t, (blended,), token, total)
        return finish, token, total

    def blend(blocks, diag):
        outs = jax.ShapeDtypeStruct(blocks.shape, BF16)
        return call(functools.partial(blend_kernel, ly), outs, (len(blocks) * unit, 2**22), blocks, diag)

    results = (field_t, field_t, jax.ShapeDtypeStruct(light_p.shape, BF16))
    source, field, light_p = call(
        first_kernel, results, (2 * unit, 2**20), order, rhs, light_p,
        far=(0, 1, 2),
        scratch=(
            pltpu.VMEM(order.shape, jnp.int32),
            pltpu.VMEM(rhs.shape, BF16),
            pltpu.SemaphoreType.DMA((3,)),
        ),
    )

    def load(hops):
        return call(
            functools.partial(load_kernel, axes), (blended_t, blended_t), (0, 2**22), hops, far=(0,),
            scratch=(pltpu.SemaphoreType.DMA((8,)),),
        )

    local, remote = load(light_h)
    blended = blend(remote, light_p)
    both = blend(current[None], charm_p)[0]
    ahead = blend(blended, both)
    next_local, next_remote = load(charm_h)
    finish, token, total = sweeps(local, blended, light_p, source, field, (both, next_local))
    start = call(functools.partial(settle_kernel, ly), total_t, (unit, 2**20), both, total)
    field = finish(add_kernel, field_t, (ahead,), token, start)
    light = finish(add_kernel, field_t, (blended,), field, total)
    local, blended = next_local, blend(next_remote, charm_p)
    over_t = (
        jax.ShapeDtypeStruct((2 * ly * cols, lx * comps), BF16),
        jax.ShapeDtypeStruct((lx, 2 * ly * cols, comps), BF16),
    )
    whole, over = call(turn_over_kernel, over_t, (unit, 2**20), light)
    out_t = jax.ShapeDtypeStruct((lx, ly, comps, wide), BF16)
    light_out, left_light = call(leave_kernel, (out_t, token_t), (unit, 2**21), light)
    finish, token, total = sweeps(local, blended, charm_p, (current, light), field, (left_light,))
    adjoint_t = jax.ShapeDtypeStruct((4, 2 * ly * cols, lx * comps), BF16)
    adjoint = call(functools.partial(adjoint_kernel, ly), adjoint_t, (4 * unit, 2**21), over, blended)
    part_t = jax.ShapeDtypeStruct((cols // 2, ly * cols), F32)
    part = finish(gram_kernel, part_t, (whole, adjoint), token, total)
    seq = finish(add_kernel, field_t, (blended,), part, total)
    seq_out, token = call(leave_kernel, (out_t, token_t), (unit, 2**21), seq)
    site_count = lx * ly * lax.axis_size("space") * lax.axis_size("tm")
    factor = 1.0 / math.sqrt(site_count * comps)

    def last(value, *got):
        ordered = in_order(got, jnp.zeros(token_t.shape, F32))
        margin_t = jax.ShapeDtypeStruct((2, cols, cols), F32)
        return call(functools.partial(margin_kernel, factor), margin_t, (2**14, 2**14), token, ordered, value, *got)

    margin = total_sum(part, last, (token,))
    return light_out.reshape(right_side.shape), seq_out.reshape(right_side.shape), margin


def solution(mesh):
    site = P("tm", "space", None, None, None, None)
    hops = P(None, "tm", "space", None, None, None, None)
    return jax.shard_map(
        body,
        mesh=mesh,
        in_specs=(site, P(), site, hops, site, hops, site),
        out_specs=(site, site, P()),
        check_vma=False,
    )
```

```python
import functools
import math

import jax
import jax.numpy as jnp
from jax import lax
from jax.experimental import pallas as pl
from jax.experimental.pallas import tpu as pltpu
from jax.sharding import PartitionSpec as P

SWEEPS = 4
F32 = jnp.float32
BF16 = jnp.bfloat16
VMEM = pl.BlockSpec(memory_space=pltpu.VMEM)
HBM = pl.BlockSpec(memory_space=pltpu.HBM)


def dot(a, b):
    return jnp.dot(a, b, preferred_element_type=F32)


def widen(field):
    half = field.shape[1] // 2
    re, im = field[:, :half], field[:, half:]
    return jnp.concatenate(
        [field, jnp.concatenate([-im, re], axis=1)], axis=0
    )


def pick(product, sites):
    rows = product.shape[0] // sites
    half = product.shape[1] // 2
    lane = lax.broadcasted_iota(jnp.int32, (rows, 2 * half), 1) % half
    out = product[:rows]
    for y in range(1, sites):
        out = jnp.where(lane >= y * (half // sites), product[y * rows : (y + 1) * rows], out)
    return out


def turn(field, shift):
    half = field.shape[1] // 2
    re, im = field[:, :half].astype(F32), field[:, half:].astype(F32)
    return jnp.concatenate(
        [pltpu.roll(re, shift % half, 1), pltpu.roll(im, shift % half, 1)], axis=1
    ).astype(field.dtype)


def toward(axes):
    odd = [lax.rem(lax.axis_index(name), 2) if paired else 0 for name, paired in axes]
    return 4 + odd[0], 5 - odd[0], 6 + odd[1], 7 - odd[1]


def hop_loads(axes, hops, local, remote, sems):
    loads = [pltpu.make_async_copy(hops.at[e], local.at[e], sems.at[e]) for e in range(4)]
    return loads + [
        pltpu.make_async_copy(hops.at[e], remote.at[n], sems.at[4 + n]) for n, e in enumerate(toward(axes))
    ]


def load_kernel(axes, hops, local, remote, sems):
    loads = hop_loads(axes, hops, local, remote, sems)
    for load in loads:
        load.start()
    for load in loads:
        load.wait()


def first_kernel(order_hbm, rhs_hbm, diag_hbm, source, out, diag, order, rhs, sems):
    copies = [
        pltpu.make_async_copy(order_hbm, order, sems.at[0]),
        pltpu.make_async_copy(rhs_hbm, rhs, sems.at[1]),
        pltpu.make_async_copy(diag_hbm, diag, sems.at[2]),
    ]
    for copy in copies:
        copy.start()
    lx, ly = rhs.shape[0], rhs.shape[1]
    cols = order.shape[1]
    half = ly * cols
    row = lax.broadcasted_iota(jnp.int32, (2 * cols, 2 * half), 0)
    lane = lax.broadcasted_iota(jnp.int32, (2 * cols, 2 * half), 1)
    copies[0].wait()
    wanted = jnp.concatenate([order[...]] * (2 * ly), axis=1)
    wanted = wanted + jnp.where(lane >= half, cols, 0)
    site = (lane % half) // cols
    hot = row == wanted
    places = [jnp.where(hot & (site == y), 1.0, 0.0).astype(BF16) for y in range(ly)]
    copies[1].wait()
    fields = []
    for x in range(lx):
        field = dot(rhs[x, 0], places[0])
        for y in range(1, ly):
            field = field + dot(rhs[x, y], places[y])
        fields.append(field.astype(BF16))
        source[x] = fields[x]
    copies[2].wait()
    for x in range(lx):
        out[x] = pick(dot(diag[x], widen(fields[x])), ly).astype(BF16)


def local_kernel(sites, hops, source, field, residue):
    lx = field.shape[0]
    cols = field.shape[2] // (2 * sites)
    for x in range(lx):
        here = field[x]
        right = jnp.concatenate(
            [
                widen(field[(x + 1) % lx]),
                widen(field[(x - 1) % lx]),
                widen(turn(here, -cols)),
                widen(turn(here, cols)),
            ],
            axis=0,
        )
        left = jnp.concatenate([hops[e, x] for e in range(4)], axis=1)
        residue[x] = (source[x].astype(F32) + pick(dot(left, right), sites)).astype(BF16)


def times_i(wide):
    row = lax.broadcasted_iota(jnp.int32, (wide, wide), 0)
    lane = lax.broadcasted_iota(jnp.int32, (wide, wide), 1)
    half = wide // 2
    return jnp.where(row == lane - half, 1.0, jnp.where(row == lane + half, -1.0, 0.0)).astype(BF16)


def blend_kernel(sites, remote, diag, out):
    count = remote.shape[0]
    lx, rows, wide = diag.shape
    comps = rows // sites
    move = times_i(wide)
    step = 2 if count % 2 == 0 else 1
    for e in range(0, count, step):
        for x in range(lx):
            blocks = [remote[e + n, x] for n in range(step)]
            lower = [dot(block, move).astype(BF16) for block in blocks]
            for y in range(sites):
                at = slice(y * comps, (y + 1) * comps)
                right = jnp.concatenate(
                    [
                        jnp.concatenate([block[at] for block in blocks], axis=1),
                        jnp.concatenate([block[at] for block in lower], axis=1),
                    ],
                    axis=0,
                )
                product = dot(diag[x, at], right).astype(BF16)
                for n in range(step):
                    out[e + n, x, at] = product[:, n * wide : (n + 1) * wide]


def settle_kernel(sites, diag, residue, total):
    for x in range(residue.shape[0]):
        total[x] = pick(dot(diag[x], widen(residue[x].astype(BF16))), sites)


def after_kernel(_, token, out):
    out[...] = token[...]


def add_kernel(sites, places, blended, token, total, *refs):
    fields, out = refs[:-1], refs[-1]
    for x in range(out.shape[0]):
        right = jnp.concatenate([widen(f[x]) for f in fields], axis=0)
        left = jnp.concatenate([blended[n, x] for n in places], axis=1)
        out[x] = (total[x] + pick(dot(left, right), sites)).astype(BF16)


def adjoint_kernel(sites, over, blended, out):
    width = over.shape[1]
    count, lx, rows, wide = blended.shape
    comps = rows // sites
    row = lax.broadcasted_iota(jnp.int32, (comps, rows), 0)
    spread = jnp.where(row == lax.broadcasted_iota(jnp.int32, (comps, rows), 1) % comps, 1.0, 0.0).astype(BF16)
    half = width // 2
    site = lax.broadcasted_iota(jnp.int32, (width, rows), 0) % half // (half // sites)
    own = site == lax.broadcasted_iota(jnp.int32, (width, rows), 1) // comps
    low = lax.broadcasted_iota(jnp.int32, (half, wide), 1) < comps
    for x in range(0, lx, 2):
        blocks = [jnp.where(own, dot(over[x + k], spread), 0.0).astype(BF16) for k in range(2)]
        at = slice(x // 2 * wide, (x // 2 + 1) * wide)
        for n in range(count):
            one, two = (dot(blocks[k], blended[n, x + k]) for k in range(2))
            re = jnp.where(low, one[:half] + pltpu.roll(one[half:], comps, 1), pltpu.roll(two[:half], comps, 1) + two[half:])
            im = jnp.where(low, one[half:] - pltpu.roll(one[:half], comps, 1), pltpu.roll(two[half:], comps, 1) - two[:half])
            out[n, :half, at] = re.astype(BF16)
            out[n, half:, at] = im.astype(BF16)


def base_kernel(sites, whole, total, out):
    total = total[...].astype(BF16)
    out[...] = packed_gram(sites, whole[...], total.reshape(-1, total.shape[2]))


def gram_kernel(sites, places, adjoint, token, base, *refs):
    fields, out = refs[:-1], refs[-1]
    left = jnp.concatenate([adjoint[n] for n in places], axis=1)
    right = jnp.concatenate([f[...].reshape(-1, f.shape[2]) for f in fields], axis=0)
    out[...] = base[...] + packed_gram(sites, left, right)


def insert_kernel(sites, current, field, source):
    for x in range(source.shape[0]):
        source[x] = pick(dot(current[x], widen(field[x])), sites).astype(BF16)


def turn_over_kernel(field, whole, out):
    lx, comps, width = field.shape
    whole[...] = field[...].reshape(lx * comps, width).astype(F32).T.astype(BF16)
    for x in range(lx):
        out[x] = field[x].astype(F32).T.astype(BF16)


def leave_kernel(*refs):
    refs, token = refs[:-1], refs[-1]
    token[...] = jnp.zeros_like(token)
    count = len(refs) // 2
    lx, ly, comps, wide = refs[count].shape
    half = refs[0].shape[2] // 2
    cols = wide // 2
    row = lax.broadcasted_iota(jnp.int32, (2 * half, wide), 0)
    lane = lax.broadcasted_iota(jnp.int32, (2 * half, wide), 1)
    start = jnp.where(lane >= cols, half - cols, 0)
    for field, out in zip(refs[:count], refs[count:], strict=True):
        whole = field[...].reshape(lx * comps, 2 * half)
        for y in range(ly):
            place = jnp.where(row == lane + start + y * cols, 1.0, 0.0).astype(BF16)
            out[:, y] = dot(whole, place).astype(BF16).reshape(lx, comps, wide)


def packed_gram(sites, left, right):
    half = left.shape[0] // 2
    cols = half // sites
    full = dot(left, right)
    real = full[:half, :half] + full[half:, half:]
    imag = full[:half, half:] - full[half:, :half]
    group = lax.broadcasted_iota(jnp.int32, (cols, half), 1) // cols
    sums = []
    for m in (real, imag):
        folded = m[:cols]
        for y in range(1, sites):
            folded = jnp.where(group == y, m[y * cols : (y + 1) * cols], folded)
        total = folded
        for y in range(1, sites):
            total = total + pltpu.roll(folded, y * cols, 1)
        sums.append(total)
    top = group[: cols // 2]
    packed = jnp.where(top == 0, sums[0][: cols // 2], sums[1][: cols // 2])
    packed = jnp.where(top == 2, sums[0][cols // 2 :], packed)
    return jnp.where(top == 3, sums[1][cols // 2 :], packed)


def margin_kernel(factor, _, token, *refs):
    out = refs[-1]
    cols = out.shape[1]
    scaled = sum([ref[...] for ref in refs[1:-1]], refs[0][...]) * factor
    for part in range(4):
        rows = slice(part // 2 * (cols // 2), (part // 2 + 1) * (cols // 2))
        out[part % 2, rows] = (pltpu.roll(scaled, scaled.shape[1] - part * cols, 1) if part else scaled)[:, :cols]


def call(kernel, outs, cost, *args, far=(), scratch=()):
    flops, moved = cost
    args = [pltpu.with_memory_space_constraint(a, pltpu.HBM) if i in far else a for i, a in enumerate(args)]
    return pl.pallas_call(
        kernel,
        out_shape=outs,
        in_specs=[HBM if i in far else VMEM for i in range(len(args))],
        out_specs=jax.tree.map(lambda _: VMEM, outs),
        scratch_shapes=scratch,
        compiler_params=pltpu.CompilerParams(vmem_limit_bytes=24 * 2**20),
        cost_estimate=pl.CostEstimate(flops=flops, bytes_accessed=moved, transcendentals=0),
    )(*args)


def in_order(arrivals, token):
    for arrived in arrivals:
        token = call(after_kernel, jax.ShapeDtypeStruct(token.shape, token.dtype), (0, 2**24), arrived, token)
    return token


def sum_kernel(token, value, *refs):
    total = value[...]
    for ref in refs[:-1]:
        total = total + ref[...]
    refs[-1][...] = total


def add_up(value, got, aside):
    token = in_order((*aside, *got), jnp.zeros((8, 128), F32))
    return call(sum_kernel, jax.ShapeDtypeStruct(value.shape, F32), (0, 2**14), token, value, *got)


def swaps(axis):
    count = lax.axis_size(axis)
    if count % 2:
        return (
            [(i, (i - 1) % count) for i in range(count)],
            [(i, (i + 1) % count) for i in range(count)],
        )
    near = [(i, i ^ 1) for i in range(count)]
    far = [(i, (i + 1 if i % 2 else i - 1) % count) for i in range(count)]
    return near, far


def total_sum(value, last, aside):
    spaces, times = lax.axis_size("space"), lax.axis_size("tm")
    if (spaces & (spaces - 1)) or (times & (times - 1)):
        return last(lax.psum(value, ("space", "tm")))

    def swap(mask):
        target = [(s ^ mask[0]) * times + (t ^ mask[1]) for s in range(spaces) for t in range(times)]
        return lax.ppermute(value, ("space", "tm"), list(enumerate(target)))

    cross = 1 if times > 1 else 0
    steps = [(0, 1 << k) for k in range(1, times.bit_length() - 1)]
    steps[1:1] = [(1 << k, 0) for k in range(spaces.bit_length() - 1)]
    groups = []
    for k in range(0, len(steps), 2):
        pair = steps[k : k + 2]
        if len(pair) == 2:
            pair.append((pair[0][0] ^ pair[1][0], pair[0][1] ^ pair[1][1]))
        groups.append([(s, t ^ cross) for s, t in reversed(pair)])
    if cross:
        groups.insert(0, [(0, 1)])
    for group in groups[:-1]:
        value = add_up(value, [swap(mask) for mask in group], aside if group == groups[-2] else ())
    return last(value, *[swap(mask) for mask in groups[-1]]) if groups else last(value)


def body(right_side, batch_order, light_diag, light_hops, charm_diag, charm_hops, current_blocks):
    lt, lz, lx, ly, comps, wide = right_side.shape
    assert lt == 1 and lz == 1
    cols = wide // 2
    rows = ly * comps
    rhs = right_side.reshape(lx, ly, comps, wide)
    order = batch_order.reshape(1, cols)
    light_p, charm_p, current = (a.reshape(lx, rows, 2 * comps) for a in (light_diag, charm_diag, current_blocks))
    light_h, charm_h = (a.reshape(8, lx, rows, 2 * comps) for a in (light_hops, charm_hops))
    shape = (lx, comps, 2 * ly * cols)
    field_t = jax.ShapeDtypeStruct(shape, BF16)
    total_t = jax.ShapeDtypeStruct(shape, F32)
    axes = tuple((name, lax.axis_size(name) % 2 == 0) for name in ("space", "tm"))
    unit = 2 * lx * rows * 2 * comps * 2 * ly * cols

    blended_t = jax.ShapeDtypeStruct((4, lx, rows, 2 * comps), BF16)
    near_s, far_s = swaps("space")
    near_t, far_t = swaps("tm")

    token_t = jax.ShapeDtypeStruct((8, 128), F32)

    def sweeps(local, blended, diag, source, field, aside={}):
        token = jnp.zeros(token_t.shape, F32)
        for left in reversed(range(SWEEPS - 1)):
            y = lax.ppermute(field, "tm", far_t)
            c = lax.ppermute(field, "tm", near_t)
            w = lax.ppermute(field, "space", far_s)
            e = lax.ppermute(field, "space", near_s)
            if not isinstance(source, jax.Array):
                source = call(functools.partial(insert_kernel, ly), field_t, (unit, 2**20), *source)
            residue = call(functools.partial(local_kernel, ly), field_t, (4 * unit, 2**21), local, source, field)
            total = call(functools.partial(settle_kernel, ly), total_t, (unit, 2**20), diag, residue)
            token = in_order((*aside.get(left, ()), e, w), token)

            def finish(kernel, outs, matrices, token, total, got=(e, w, y, c)):
                return call(
                    functools.partial(kernel, ly, (0, 1, 3, 2)), outs, (4 * unit, 2**20), *matrices, token, total, *got
                )

            if left:
                field = finish(add_kernel, field_t, (blended,), token, total)
        return finish, token, total

    def blend(blocks, diag):
        outs = jax.ShapeDtypeStruct(blocks.shape, BF16)
        return call(functools.partial(blend_kernel, ly), outs, (len(blocks) * unit, 2**22), blocks, diag)

    results = (field_t, field_t, jax.ShapeDtypeStruct(light_p.shape, BF16))
    source, field, light_p = call(
        first_kernel, results, (2 * unit, 2**20), order, rhs, light_p,
        far=(0, 1, 2),
        scratch=(
            pltpu.VMEM(order.shape, jnp.int32),
            pltpu.VMEM(rhs.shape, BF16),
            pltpu.SemaphoreType.DMA((3,)),
        ),
    )

    def load(hops):
        return call(
            functools.partial(load_kernel, axes), (blended_t, blended_t), (0, 2**22), hops, far=(0,),
            scratch=(pltpu.SemaphoreType.DMA((8,)),),
        )

    local, remote = load(light_h)
    blended = blend(remote, light_p)
    both = blend(current[None], charm_p)[0]
    ahead = blend(blended, both)
    next_local, next_remote = load(charm_h)
    finish, token, total = sweeps(local, blended, light_p, source, field, {1: (both, next_local)})
    start = call(functools.partial(settle_kernel, ly), total_t, (unit, 2**20), both, total)
    field = finish(add_kernel, field_t, (ahead,), token, start)
    light = finish(add_kernel, field_t, (blended,), field, total)
    local, blended = next_local, blend(next_remote, charm_p)
    over_t = (
        jax.ShapeDtypeStruct((2 * ly * cols, lx * comps), BF16),
        jax.ShapeDtypeStruct((lx, 2 * ly * cols, comps), BF16),
    )
    whole, over = call(turn_over_kernel, over_t, (unit, 2**20), light)
    out_t = jax.ShapeDtypeStruct((lx, ly, comps, wide), BF16)
    light_out, left_light = call(leave_kernel, (out_t, token_t), (unit, 2**21), light)
    adjoint_t = jax.ShapeDtypeStruct((4, 2 * ly * cols, lx * comps), BF16)
    adjoint = call(functools.partial(adjoint_kernel, ly), adjoint_t, (4 * unit, 2**21), over, blended)
    finish, token, total = sweeps(local, blended, charm_p, (current, light), field, {1: (adjoint,), 0: (left_light,)})
    part_t = jax.ShapeDtypeStruct((cols // 2, ly * cols), F32)
    base = call(functools.partial(base_kernel, ly), part_t, (unit, 2**20), whole, total)
    part = finish(gram_kernel, part_t, (adjoint,), token, base)
    seq = finish(add_kernel, field_t, (blended,), part, total)
    seq_out, token = call(leave_kernel, (out_t, token_t), (unit, 2**21), seq)
    site_count = lx * ly * lax.axis_size("space") * lax.axis_size("tm")
    factor = 1.0 / math.sqrt(site_count * comps)

    def last(value, *got):
        ordered = in_order(got, jnp.zeros(token_t.shape, F32))
        margin_t = jax.ShapeDtypeStruct((2, cols, cols), F32)
        return call(functools.partial(margin_kernel, factor), margin_t, (2**14, 2**14), token, ordered, value, *got)

    margin = total_sum(part, last, (token,))
    return light_out.reshape(right_side.shape), seq_out.reshape(right_side.shape), margin


def solution(mesh):
    site = P("tm", "space", None, None, None, None)
    hops = P(None, "tm", "space", None, None, None, None)
    return jax.shard_map(
        body,
        mesh=mesh,
        in_specs=(site, P(), site, hops, site, hops, site),
        out_specs=(site, site, P()),
        check_vma=False,
    )
```

```python
import functools
import math

import jax
import jax.numpy as jnp
from jax import lax
from jax.experimental import pallas as pl
from jax.experimental.pallas import tpu as pltpu
from jax.sharding import PartitionSpec as P

SWEEPS = 4
F32 = jnp.float32
BF16 = jnp.bfloat16
VMEM = pl.BlockSpec(memory_space=pltpu.VMEM)
HBM = pl.BlockSpec(memory_space=pltpu.HBM)


def dot(a, b):
    return jnp.dot(a, b, preferred_element_type=F32)


def widen(field):
    half = field.shape[1] // 2
    re, im = field[:, :half], field[:, half:]
    return jnp.concatenate(
        [field, jnp.concatenate([-im, re], axis=1)], axis=0
    )


def pick(product, sites):
    rows = product.shape[0] // sites
    half = product.shape[1] // 2
    lane = lax.broadcasted_iota(jnp.int32, (rows, 2 * half), 1) % half
    out = product[:rows]
    for y in range(1, sites):
        out = jnp.where(lane >= y * (half // sites), product[y * rows : (y + 1) * rows], out)
    return out


def turn(field, shift):
    half = field.shape[1] // 2
    re, im = field[:, :half].astype(F32), field[:, half:].astype(F32)
    return jnp.concatenate(
        [pltpu.roll(re, shift % half, 1), pltpu.roll(im, shift % half, 1)], axis=1
    ).astype(field.dtype)


def toward(axes):
    odd = [lax.rem(lax.axis_index(name), 2) if paired else 0 for name, paired in axes]
    return 4 + odd[0], 5 - odd[0], 6 + odd[1], 7 - odd[1]


def hop_loads(axes, hops, local, remote, sems):
    loads = [pltpu.make_async_copy(hops.at[e], local.at[e], sems.at[e]) for e in range(4)]
    return loads + [
        pltpu.make_async_copy(hops.at[e], remote.at[n], sems.at[4 + n]) for n, e in enumerate(toward(axes))
    ]


def load_kernel(axes, hops, local, remote, sems):
    loads = hop_loads(axes, hops, local, remote, sems)
    for load in loads:
        load.start()
    for load in loads:
        load.wait()


def first_kernel(order_hbm, rhs_hbm, diag_hbm, source, out, diag, order, rhs, sems):
    copies = [
        pltpu.make_async_copy(order_hbm, order, sems.at[0]),
        pltpu.make_async_copy(rhs_hbm, rhs, sems.at[1]),
        pltpu.make_async_copy(diag_hbm, diag, sems.at[2]),
    ]
    for copy in copies:
        copy.start()
    lx, ly = rhs.shape[0], rhs.shape[1]
    cols = order.shape[1]
    half = ly * cols
    row = lax.broadcasted_iota(jnp.int32, (2 * cols, 2 * half), 0)
    lane = lax.broadcasted_iota(jnp.int32, (2 * cols, 2 * half), 1)
    copies[0].wait()
    wanted = jnp.concatenate([order[...]] * (2 * ly), axis=1)
    wanted = wanted + jnp.where(lane >= half, cols, 0)
    site = (lane % half) // cols
    hot = row == wanted
    places = [jnp.where(hot & (site == y), 1.0, 0.0).astype(BF16) for y in range(ly)]
    copies[1].wait()
    fields = []
    for x in range(lx):
        field = dot(rhs[x, 0], places[0])
        for y in range(1, ly):
            field = field + dot(rhs[x, y], places[y])
        fields.append(field.astype(BF16))
        source[x] = fields[x]
    copies[2].wait()
    for x in range(lx):
        out[x] = pick(dot(diag[x], widen(fields[x])), ly).astype(BF16)


def local_kernel(sites, hops, source, field, residue):
    lx = field.shape[0]
    cols = field.shape[2] // (2 * sites)
    for x in range(lx):
        here = field[x]
        right = jnp.concatenate(
            [
                widen(field[(x + 1) % lx]),
                widen(field[(x - 1) % lx]),
                widen(turn(here, -cols)),
                widen(turn(here, cols)),
            ],
            axis=0,
        )
        left = jnp.concatenate([hops[e, x] for e in range(4)], axis=1)
        residue[x] = (source[x].astype(F32) + pick(dot(left, right), sites)).astype(BF16)


def rest_kernel(sites, hops, diag, source, field, total, residue):
    local_kernel(sites, hops, source, field, residue)
    settle_kernel(sites, diag, residue, total)


def times_i(wide):
    row = lax.broadcasted_iota(jnp.int32, (wide, wide), 0)
    lane = lax.broadcasted_iota(jnp.int32, (wide, wide), 1)
    half = wide // 2
    return jnp.where(row == lane - half, 1.0, jnp.where(row == lane + half, -1.0, 0.0)).astype(BF16)


def blend_kernel(sites, remote, diag, out):
    count = remote.shape[0]
    lx, rows, wide = diag.shape
    comps = rows // sites
    move = times_i(wide)
    step = 2 if count % 2 == 0 else 1
    for e in range(0, count, step):
        for x in range(lx):
            blocks = [remote[e + n, x] for n in range(step)]
            lower = [dot(block, move).astype(BF16) for block in blocks]
            for y in range(sites):
                at = slice(y * comps, (y + 1) * comps)
                right = jnp.concatenate(
                    [
                        jnp.concatenate([block[at] for block in blocks], axis=1),
                        jnp.concatenate([block[at] for block in lower], axis=1),
                    ],
                    axis=0,
                )
                product = dot(diag[x, at], right).astype(BF16)
                for n in range(step):
                    out[e + n, x, at] = product[:, n * wide : (n + 1) * wide]


def settle_kernel(sites, diag, residue, total):
    for x in range(residue.shape[0]):
        total[x] = pick(dot(diag[x], widen(residue[x].astype(BF16))), sites)


def after_kernel(_, token, out):
    out[...] = token[...]


def add_kernel(sites, places, blended, token, total, *refs):
    fields, out = refs[:-1], refs[-1]
    for x in range(out.shape[0]):
        right = jnp.concatenate([widen(f[x]) for f in fields], axis=0)
        left = jnp.concatenate([blended[n, x] for n in places], axis=1)
        out[x] = (total[x] + pick(dot(left, right), sites)).astype(BF16)


def adjoint_kernel(sites, over, blended, out):
    width = over.shape[1]
    count, lx, rows, wide = blended.shape
    comps = rows // sites
    row = lax.broadcasted_iota(jnp.int32, (comps, rows), 0)
    spread = jnp.where(row == lax.broadcasted_iota(jnp.int32, (comps, rows), 1) % comps, 1.0, 0.0).astype(BF16)
    half = width // 2
    site = lax.broadcasted_iota(jnp.int32, (width, rows), 0) % half // (half // sites)
    own = site == lax.broadcasted_iota(jnp.int32, (width, rows), 1) // comps
    low = lax.broadcasted_iota(jnp.int32, (half, wide), 1) < comps
    for x in range(0, lx, 2):
        blocks = [jnp.where(own, dot(over[x + k], spread), 0.0).astype(BF16) for k in range(2)]
        at = slice(x // 2 * wide, (x // 2 + 1) * wide)
        for n in range(count):
            one, two = (dot(blocks[k], blended[n, x + k]) for k in range(2))
            re = jnp.where(low, one[:half] + pltpu.roll(one[half:], comps, 1), pltpu.roll(two[:half], comps, 1) + two[half:])
            im = jnp.where(low, one[half:] - pltpu.roll(one[:half], comps, 1), pltpu.roll(two[half:], comps, 1) - two[:half])
            out[n, :half, at] = re.astype(BF16)
            out[n, half:, at] = im.astype(BF16)


def gram_kernel(sites, places, whole, adjoint, token, total, *refs):
    fields, out = refs[:-1], refs[-1]
    left = jnp.concatenate([whole[...]] + [adjoint[n] for n in places], axis=1)
    right = [total[...].astype(BF16)] + [f[...] for f in fields]
    right = jnp.concatenate([f.reshape(-1, f.shape[2]) for f in right], axis=0)
    out[...] = packed_gram(sites, left, right)


def insert_kernel(sites, current, field, source):
    for x in range(source.shape[0]):
        source[x] = pick(dot(current[x], widen(field[x])), sites).astype(BF16)


def turn_over_kernel(field, whole, out):
    lx, comps, width = field.shape
    whole[...] = field[...].reshape(lx * comps, width).astype(F32).T.astype(BF16)
    for x in range(lx):
        out[x] = field[x].astype(F32).T.astype(BF16)


def leave_kernel(*refs):
    refs, token = refs[:-1], refs[-1]
    token[...] = jnp.zeros_like(token)
    count = len(refs) // 2
    lx, ly, comps, wide = refs[count].shape
    half = refs[0].shape[2] // 2
    cols = wide // 2
    row = lax.broadcasted_iota(jnp.int32, (2 * half, wide), 0)
    lane = lax.broadcasted_iota(jnp.int32, (2 * half, wide), 1)
    start = jnp.where(lane >= cols, half - cols, 0)
    for field, out in zip(refs[:count], refs[count:], strict=True):
        whole = field[...].reshape(lx * comps, 2 * half)
        for y in range(ly):
            place = jnp.where(row == lane + start + y * cols, 1.0, 0.0).astype(BF16)
            out[:, y] = dot(whole, place).astype(BF16).reshape(lx, comps, wide)


def packed_gram(sites, left, right):
    half = left.shape[0] // 2
    cols = half // sites
    full = dot(left, right)
    real = full[:half, :half] + full[half:, half:]
    imag = full[:half, half:] - full[half:, :half]
    group = lax.broadcasted_iota(jnp.int32, (cols, half), 1) // cols
    sums = []
    for m in (real, imag):
        folded = m[:cols]
        for y in range(1, sites):
            folded = jnp.where(group == y, m[y * cols : (y + 1) * cols], folded)
        total = folded
        for y in range(1, sites):
            total = total + pltpu.roll(folded, y * cols, 1)
        sums.append(total)
    top = group[: cols // 2]
    packed = jnp.where(top == 0, sums[0][: cols // 2], sums[1][: cols // 2])
    packed = jnp.where(top == 2, sums[0][cols // 2 :], packed)
    return jnp.where(top == 3, sums[1][cols // 2 :], packed)


def margin_kernel(factor, _, token, *refs):
    out = refs[-1]
    cols = out.shape[1]
    scaled = sum([ref[...] for ref in refs[1:-1]], refs[0][...]) * factor
    for part in range(4):
        rows = slice(part // 2 * (cols // 2), (part // 2 + 1) * (cols // 2))
        out[part % 2, rows] = (pltpu.roll(scaled, scaled.shape[1] - part * cols, 1) if part else scaled)[:, :cols]


def call(kernel, outs, cost, *args, far=(), scratch=()):
    flops, moved = cost
    args = [pltpu.with_memory_space_constraint(a, pltpu.HBM) if i in far else a for i, a in enumerate(args)]
    return pl.pallas_call(
        kernel,
        out_shape=outs,
        in_specs=[HBM if i in far else VMEM for i in range(len(args))],
        out_specs=jax.tree.map(lambda _: VMEM, outs),
        scratch_shapes=scratch,
        compiler_params=pltpu.CompilerParams(vmem_limit_bytes=24 * 2**20),
        cost_estimate=pl.CostEstimate(flops=flops, bytes_accessed=moved, transcendentals=0),
    )(*args)


def in_order(arrivals, token):
    for arrived in arrivals:
        token = call(after_kernel, jax.ShapeDtypeStruct(token.shape, token.dtype), (0, 2**24), arrived, token)
    return token


def sum_kernel(token, value, *refs):
    total = value[...]
    for ref in refs[:-1]:
        total = total + ref[...]
    refs[-1][...] = total


def add_up(value, got, aside):
    token = in_order((*aside, *got), jnp.zeros((8, 128), F32))
    return call(sum_kernel, jax.ShapeDtypeStruct(value.shape, F32), (0, 2**14), token, value, *got)


def swaps(axis):
    count = lax.axis_size(axis)
    if count % 2:
        return (
            [(i, (i - 1) % count) for i in range(count)],
            [(i, (i + 1) % count) for i in range(count)],
        )
    near = [(i, i ^ 1) for i in range(count)]
    far = [(i, (i + 1 if i % 2 else i - 1) % count) for i in range(count)]
    return near, far


def total_sum(value, last, aside):
    spaces, times = lax.axis_size("space"), lax.axis_size("tm")
    if (spaces & (spaces - 1)) or (times & (times - 1)):
        return last(lax.psum(value, ("space", "tm")))

    def swap(mask):
        target = [(s ^ mask[0]) * times + (t ^ mask[1]) for s in range(spaces) for t in range(times)]
        return lax.ppermute(value, ("space", "tm"), list(enumerate(target)))

    cross = 1 if times > 1 else 0
    steps = [(0, 1 << k) for k in range(1, times.bit_length() - 1)]
    steps[1:1] = [(1 << k, 0) for k in range(spaces.bit_length() - 1)]
    groups = []
    for k in range(0, len(steps), 2):
        pair = steps[k : k + 2]
        if len(pair) == 2:
            pair.append((pair[0][0] ^ pair[1][0], pair[0][1] ^ pair[1][1]))
        groups.append([(s, t ^ cross) for s, t in reversed(pair)])
    if cross:
        groups.insert(1, [(0, 1)])
    for group in groups[:-1]:
        value = add_up(value, [swap(mask) for mask in group], aside if group == groups[0] else ())
    return last(value, *[swap(mask) for mask in groups[-1]]) if groups else last(value)


def body(right_side, batch_order, light_diag, light_hops, charm_diag, charm_hops, current_blocks):
    lt, lz, lx, ly, comps, wide = right_side.shape
    assert lt == 1 and lz == 1
    cols = wide // 2
    rows = ly * comps
    rhs = right_side.reshape(lx, ly, comps, wide)
    order = batch_order.reshape(1, cols)
    light_p, charm_p, current = (a.reshape(lx, rows, 2 * comps) for a in (light_diag, charm_diag, current_blocks))
    light_h, charm_h = (a.reshape(8, lx, rows, 2 * comps) for a in (light_hops, charm_hops))
    shape = (lx, comps, 2 * ly * cols)
    field_t = jax.ShapeDtypeStruct(shape, BF16)
    total_t = jax.ShapeDtypeStruct(shape, F32)
    axes = tuple((name, lax.axis_size(name) % 2 == 0) for name in ("space", "tm"))
    unit = 2 * lx * rows * 2 * comps * 2 * ly * cols

    blended_t = jax.ShapeDtypeStruct((4, lx, rows, 2 * comps), BF16)
    near_s, far_s = swaps("space")
    near_t, far_t = swaps("tm")

    token_t = jax.ShapeDtypeStruct((8, 128), F32)

    def sweeps(local, blended, diag, source, field, aside=()):
        token = jnp.zeros(token_t.shape, F32)
        for left in reversed(range(SWEEPS - 1)):
            y = lax.ppermute(field, "tm", far_t)
            c = lax.ppermute(field, "tm", near_t)
            w = lax.ppermute(field, "space", far_s)
            e = lax.ppermute(field, "space", near_s)
            if not isinstance(source, jax.Array):
                source = call(functools.partial(insert_kernel, ly), field_t, (unit, 2**20), *source)
            total = call(
                functools.partial(rest_kernel, ly), total_t, (5 * unit, 2**21), local, diag, source, field,
                scratch=(pltpu.VMEM(shape, BF16),),
            )
            token = in_order((*(aside if left == 1 else ()), e, w), token)

            def finish(kernel, outs, matrices, token, total, got=(e, w, y, c)):
                return call(
                    functools.partial(kernel, ly, (0, 1, 3, 2)), outs, (4 * unit, 2**20), *matrices, token, total, *got
                )

            if left:
                field = finish(add_kernel, field_t, (blended,), token, total)
        return finish, token, total

    def blend(blocks, diag):
        outs = jax.ShapeDtypeStruct(blocks.shape, BF16)
        return call(functools.partial(blend_kernel, ly), outs, (len(blocks) * unit, 2**22), blocks, diag)

    results = (field_t, field_t, jax.ShapeDtypeStruct(light_p.shape, BF16))
    source, field, light_p = call(
        first_kernel, results, (2 * unit, 2**20), order, rhs, light_p,
        far=(0, 1, 2),
        scratch=(
            pltpu.VMEM(order.shape, jnp.int32),
            pltpu.VMEM(rhs.shape, BF16),
            pltpu.SemaphoreType.DMA((3,)),
        ),
    )

    def load(hops):
        return call(
            functools.partial(load_kernel, axes), (blended_t, blended_t), (0, 2**22), hops, far=(0,),
            scratch=(pltpu.SemaphoreType.DMA((8,)),),
        )

    local, remote = load(light_h)
    blended = blend(remote, light_p)
    both = blend(current[None], charm_p)[0]
    ahead = blend(blended, both)
    next_local, next_remote = load(charm_h)
    finish, token, total = sweeps(local, blended, light_p, source, field, (both, next_local))
    start = call(functools.partial(settle_kernel, ly), total_t, (unit, 2**20), both, total)
    field = finish(add_kernel, field_t, (ahead,), token, start)
    light = finish(add_kernel, field_t, (blended,), field, total)
    local, blended = next_local, blend(next_remote, charm_p)
    over_t = (
        jax.ShapeDtypeStruct((2 * ly * cols, lx * comps), BF16),
        jax.ShapeDtypeStruct((lx, 2 * ly * cols, comps), BF16),
    )
    whole, over = call(turn_over_kernel, over_t, (unit, 2**20), light)
    out_t = jax.ShapeDtypeStruct((lx, ly, comps, wide), BF16)
    light_out, left_light = call(leave_kernel, (out_t, token_t), (unit, 2**21), light)
    finish, token, total = sweeps(local, blended, charm_p, (current, light), field, (left_light,))
    adjoint_t = jax.ShapeDtypeStruct((4, 2 * ly * cols, lx * comps), BF16)
    adjoint = call(functools.partial(adjoint_kernel, ly), adjoint_t, (4 * unit, 2**21), over, blended)
    part_t = jax.ShapeDtypeStruct((cols // 2, ly * cols), F32)
    part = finish(gram_kernel, part_t, (whole, adjoint), token, total)
    seq = finish(add_kernel, field_t, (blended,), part, total)
    seq_out, token = call(leave_kernel, (out_t, token_t), (unit, 2**21), seq)
    site_count = lx * ly * lax.axis_size("space") * lax.axis_size("tm")
    factor = 1.0 / math.sqrt(site_count * comps)

    def last(value, *got):
        ordered = in_order(got, jnp.zeros(token_t.shape, F32))
        margin_t = jax.ShapeDtypeStruct((2, cols, cols), F32)
        return call(functools.partial(margin_kernel, factor), margin_t, (2**14, 2**14), token, ordered, value, *got)

    margin = total_sum(part, last, (token,))
    return light_out.reshape(right_side.shape), seq_out.reshape(right_side.shape), margin


def solution(mesh):
    site = P("tm", "space", None, None, None, None)
    hops = P(None, "tm", "space", None, None, None, None)
    return jax.shard_map(
        body,
        mesh=mesh,
        in_specs=(site, P(), site, hops, site, hops, site),
        out_specs=(site, site, P()),
        check_vma=False,
    )
```
